32 devices in a mesh: groups: 2 (over y), ep: 4 (over z), tp: 4 (over x, core).
Axes of the slice: x: 2, y: 2, z: 4, core: 2. Of those that a mesh axis runs over, the one named last changes fastest.
Arguments:
- tokens: bfloat16 [128, 2, 8192], P(('groups', 'ep')), parts along dimension 0, may hold values from -400 to 400
- query_weight: bfloat16 [8192, 8192], P('ep', 'tp'), may hold values from -0.0625 to 0.0625
- key_weight: bfloat16 [8192, 1024], P('ep', 'tp'), may hold values from -0.0625 to 0.0625
- value_weight: bfloat16 [8192, 1024], P('ep', 'tp'), may hold values from -0.0625 to 0.0625
- output_weight: bfloat16 [8192, 8192], P('tp', 'ep'), may hold values from -0.0625 to 0.0625
- adapter_down_maps: bfloat16 [32, 8192, 64], P('ep', 'tp'), may hold values from -0.0625 to 0.0625
- adapter_up_maps: bfloat16 [32, 64, 8192], P('ep', None, 'tp'), may hold values from -0.75 to 0.75
- rotated_cache_keys: bfloat16 [128, 128, 1024], P(('groups', 'ep'), None, 'tp'), parts along dimension 0, may hold values from -68 to 68
- cached_value_rows: bfloat16 [128, 128, 1024], P(('groups', 'ep'), None, 'tp'), parts along dimension 0, may hold values from -12 to 12
- adapter_index: int32 [128], P(('groups', 'ep')), parts along dimension 0, may hold values from 0 to 31, as said below
- cached_lengths: int32 [128], P(('groups', 'ep')), parts along dimension 0, may hold values from 1 to 128, as said below
Outputs:
- attn_out: bfloat16 [128, 2, 8192], P(('groups', 'ep')), parts along dimension 0
The draws below stay inside these ranges and needn't reach their ends.
There are 2 independent parts, one for each index of `groups`. The reference program is written for one: setup_inputs(seed, part) draws one part's arguments, and reference() takes and returns one part's arrays. A program takes and returns all parts, laid end to end along the dimension named above; an argument that names none is the same for every part. Nothing has to cross between parts.
Inputs may be any that keep to these rules, and one draw needn't show every extreme that they name: `adapter_index`: adapters a * 8 to a * 8 + 7 belong to owner a. In each aligned block of 16 requests at most 8 requests name adapters of one owner, and one owner, the same in every block, is named by exactly 8 requests of every block. `cached_lengths`: some request has 128 cached positions.
All inputs are finite; a program needn't handle non-finite values.
Results may differ from the reference program's by a relative error of at most 0.012.
The reference program's roundings to bfloat16 on the way count: a program that leaves them out, or rounds other values in their place, can miss the bound.
Values may be sent and summed in bfloat16 or wider, within the bound.
A program may use at most 128 MiB of HBM per device.

```python
import math
import jax
import jax.numpy as jnp
from jax import lax

MODEL_DIM = 8192
QUERY_HEADS = 64
KEY_HEADS = 8
HEAD_SIZE = 128
ADAPTER_RANK = 64
ADP_DEV = 8
STEPS = 2
CACHE_SLOTS = 128
REQUESTS_LOCAL = 16
CAP = 8
REQUEST_TOTAL = 64
ADAPTER_TOTAL = 32
N_EP = 4


def draw_tokens(key, part):
    key = jax.random.fold_in(key, 11)
    key_one, key_two, key_three = jax.random.split(key, 3)
    complete_shape = (REQUESTS_LOCAL * N_EP, STEPS, MODEL_DIM)
    row_scale = jnp.exp(jax.random.uniform(key_one, (REQUESTS_LOCAL * N_EP, STEPS, 1), minval=0.0, maxval=math.log(10.0)))
    column_scale = jnp.exp(jax.random.uniform(key_two, (1, 1, MODEL_DIM), minval=0.0, maxval=math.log(10.0)))
    base_draw = jax.random.normal(key_three, complete_shape)
    base_draw = jnp.clip(base_draw, -4.0, 4.0)
    return (base_draw * row_scale * column_scale).astype(jnp.bfloat16)


def draw_rotated_cache_keys(key, part):
    key = jax.random.fold_in(key, 23)
    key_one = jax.random.fold_in(key, 0)
    complete_shape = (REQUESTS_LOCAL * N_EP, CACHE_SLOTS, KEY_HEADS * HEAD_SIZE)
    base_draw = jnp.clip(jax.random.normal(key_one, complete_shape), -6.0, 6.0)
    return base_draw.astype(jnp.bfloat16)


def draw_adapter_index(key, part):
    key = jax.random.fold_in(key, 37)
    key_one, key_two, key_three = jax.random.split(key, 3)
    hot_owner = jax.random.randint(key_one, (), 0, N_EP)
    popular = jax.random.permutation(key_two, N_EP)
    copies = jnp.arange(N_EP * CAP) // CAP

    def block_draw(block_key):
        score_key, order_key, pick_key = jax.random.split(block_key, 3)
        scores = jax.random.randint(score_key, (N_EP * CAP,), 0, 4096) * (1 + popular[copies])
        scores = jnp.where(copies == hot_owner, 1 << 22, scores)
        scores = scores * (N_EP * CAP) + jnp.arange(N_EP * CAP)
        selected_rows = lax.top_k(scores, REQUESTS_LOCAL)[1] // CAP
        owners = selected_rows[jax.random.permutation(order_key, REQUESTS_LOCAL)]
        local_pick = jax.random.randint(pick_key, (REQUESTS_LOCAL,), 0, ADP_DEV)
        return owners * ADP_DEV + local_pick
    adapter_list = jax.vmap(block_draw)(jax.random.split(key_three, N_EP))
    return adapter_list.reshape(-1).astype(jnp.int32)


def draw_cached_lengths(key, part):
    key = jax.random.fold_in(key, 41)
    key_one, key_two = jax.random.split(key)
    request_count = REQUESTS_LOCAL * N_EP
    values = jax.random.randint(key_one, (request_count,), 1, CACHE_SLOTS + 1)
    longest_at = jax.random.randint(key_two, (), 0, request_count)
    return jnp.where(jnp.arange(request_count) == longest_at, CACHE_SLOTS, values).astype(jnp.int32)


def levels(key, extent, shards, smallest, high):
    factor_of, own = 1.0, jax.random.fold_in(key, 6)
    for dim, parts in shards:
        heights = jnp.exp(jax.random.uniform(jax.random.fold_in(own, dim), (parts,), jnp.float32, smallest / len(shards), high / len(shards)))
        factor_of = factor_of * jnp.repeat(heights, extent[dim] // parts).reshape([-1 if axis == dim else 1 for axis in range(len(extent))])
    return factor_of


def scatter_about(own_key, extent, spread, bound, shards=(), held_as=jnp.bfloat16):
    loudness = levels(own_key, extent, shards, -0.22, 0.18) if shards else 1.0
    values = jax.random.normal(own_key, extent, jnp.float32) * spread * loudness
    return jnp.minimum(jnp.maximum(values, -bound), bound).astype(held_as)


def setup_inputs(seed: int = 0, part: int = 0) -> dict:
    seeds = jax.random.split(jax.random.key(seed), 12)
    own_keys = jax.random.split(jax.random.fold_in(seeds[11], part), 12)
    return {
        "tokens": draw_tokens(jax.random.fold_in(jax.random.fold_in(seeds[11], part), 71), part),
        "query_weight": scatter_about(seeds[1], (MODEL_DIM, QUERY_HEADS * HEAD_SIZE), MODEL_DIM ** -0.5, 0.0625, ((0, 4), (1, 4))),
        "key_weight": scatter_about(seeds[2], (MODEL_DIM, KEY_HEADS * HEAD_SIZE), MODEL_DIM ** -0.5, 0.0625, ((0, 4), (1, 4))),
        "value_weight": scatter_about(seeds[3], (MODEL_DIM, KEY_HEADS * HEAD_SIZE), MODEL_DIM ** -0.5, 0.0625, ((0, 4), (1, 4))),
        "output_weight": scatter_about(seeds[4], (QUERY_HEADS * HEAD_SIZE, MODEL_DIM), (QUERY_HEADS * HEAD_SIZE) ** -0.5, 0.0625, ((0, 4), (1, 4))),
        "adapter_down_maps": scatter_about(seeds[5], (ADAPTER_TOTAL, MODEL_DIM, ADAPTER_RANK), MODEL_DIM ** -0.5, 0.0625, ((0, 4), (1, 4))),
        "adapter_up_maps": scatter_about(seeds[6], (ADAPTER_TOTAL, ADAPTER_RANK, QUERY_HEADS * HEAD_SIZE), ADAPTER_RANK ** -0.5, 0.75, ((0, 4), (2, 4))),
        "rotated_cache_keys": draw_rotated_cache_keys(jax.random.fold_in(jax.random.fold_in(seeds[11], part), 71), part),
        "cached_value_rows": scatter_about(own_keys[8], (REQUEST_TOTAL, CACHE_SLOTS, KEY_HEADS * HEAD_SIZE), 2.0, 12.0, ((0, 4), (2, 4))),
        "adapter_index": draw_adapter_index(jax.random.fold_in(jax.random.fold_in(seeds[11], part), 71), part),
        "cached_lengths": draw_cached_lengths(jax.random.fold_in(jax.random.fold_in(seeds[11], part), 71), part),
    }


EPSILON = 1e-05
THETA = 500000.0
MASKED = -1e+30

def normalize(tokens):
    widened = tokens.astype(jnp.float32)
    factor = lax.rsqrt(lax.optimization_barrier(jnp.mean(widened * widened, axis=-1, keepdims=True)) + EPSILON)
    return (widened * factor).astype(jnp.bfloat16)

def apply_rotation(values, token_positions):
    half_size = values.shape[-1] // 2
    pair_ranks = jnp.arange(half_size).astype(jnp.float32)
    inverse = jnp.exp(pair_ranks * (-2.0 / values.shape[-1]) * math.log(THETA))
    angles = token_positions[..., None, None] * inverse
    cosine = jnp.cos(angles)
    sine_part = jnp.sin(angles)
    lower_half = values[..., :half_size]
    upper_half = values[..., half_size:]
    return jnp.concatenate([lower_half * cosine - upper_half * sine_part, upper_half * cosine + lower_half * sine_part], axis=-1)

def attend_step(query_rows, keys_cached, values_cached, incoming_keys, incoming_values, lengths):
    score_scale = 1.0 / math.sqrt(query_rows.shape[-1])
    decode_steps = query_rows.shape[1]
    cache_len = keys_cached.shape[1]
    queries_wide = query_rows.astype(jnp.float32)
    cached = jnp.einsum('rsgmd,rcgd->rsgmc', queries_wide, keys_cached.astype(jnp.float32)) * score_scale
    fresh_scores = jnp.einsum('rsgmd,rtgd->rsgmt', queries_wide, incoming_keys.astype(jnp.float32)) * score_scale
    live_cache = (jnp.arange(cache_len)[None, :] < lengths[:, None])[:, None, None, None, :]
    live_fresh = (jnp.arange(decode_steps)[None, :] <= jnp.arange(decode_steps)[:, None])[None, :, None, None, :]
    cached = jnp.where(live_cache, cached, MASKED)
    fresh_scores = jnp.where(live_fresh, fresh_scores, MASKED)
    row_max = jnp.maximum(lax.optimization_barrier(jnp.max(cached, -1, keepdims=True)), lax.optimization_barrier(jnp.max(fresh_scores, -1, keepdims=True)))
    cached_exp = jnp.where(live_cache, jnp.exp(cached - row_max), 0.0)
    fresh_exp = jnp.where(live_fresh, jnp.exp(fresh_scores - row_max), 0.0)
    totals = lax.optimization_barrier(jnp.sum(cached_exp, -1, keepdims=True)) + lax.optimization_barrier(jnp.sum(fresh_exp, -1, keepdims=True))
    cached_weight = (cached_exp / totals).astype(jnp.bfloat16)
    fresh_weight = (fresh_exp / totals).astype(jnp.bfloat16)
    mixture = jnp.einsum('rsgmc,rcgd->rsgmd', cached_weight.astype(jnp.float32), values_cached.astype(jnp.float32))
    mixture = mixture + jnp.einsum('rsgmt,rtgd->rsgmd', fresh_weight.astype(jnp.float32), incoming_values.astype(jnp.float32))
    return mixture.astype(jnp.bfloat16).reshape(query_rows.shape[0], decode_steps, -1)

def reference(tokens, query_weight, key_weight, value_weight, output_weight, adapter_down_maps, adapter_up_maps, rotated_cache_keys, cached_value_rows, adapter_index, cached_lengths):
    request_batch, decode_steps, model_width = tokens.shape
    query_columns = QUERY_HEADS * HEAD_SIZE
    key_columns = KEY_HEADS * HEAD_SIZE
    normed = normalize(tokens)
    flat_rows = normed.reshape(request_batch * decode_steps, model_width)
    joined = jnp.concatenate([query_weight, key_weight, value_weight], axis=1)
    projected_rows = jnp.dot(flat_rows, joined, preferred_element_type=jnp.float32)

    def adapt(request_item):
        request_rows, adapter_apply = request_item
        down_weight = lax.dynamic_index_in_dim(adapter_down_maps, adapter_apply, 0, keepdims=False)
        up_weight = lax.dynamic_index_in_dim(adapter_up_maps, adapter_apply, 0, keepdims=False)
        shrunk = jnp.dot(request_rows, down_weight, preferred_element_type=jnp.float32).astype(jnp.bfloat16)
        return jnp.dot(shrunk, up_weight, preferred_element_type=jnp.float32).astype(jnp.bfloat16)
    adapter_delta = lax.map(adapt, (normed, adapter_index))
    projected_rows = projected_rows.reshape(request_batch, decode_steps, -1)
    token_positions = cached_lengths.astype(jnp.float32)[:, None] + jnp.arange(decode_steps).astype(jnp.float32)[None, :]
    query_rows = projected_rows[..., :query_columns] + adapter_delta.astype(jnp.float32)
    query_rows = apply_rotation(query_rows.reshape(request_batch, decode_steps, QUERY_HEADS, HEAD_SIZE), token_positions).astype(jnp.bfloat16)
    incoming_keys = apply_rotation(projected_rows[..., query_columns:query_columns + key_columns].reshape(request_batch, decode_steps, KEY_HEADS, HEAD_SIZE), token_positions).astype(jnp.bfloat16)
    incoming_values = projected_rows[..., query_columns + key_columns:].astype(jnp.bfloat16).reshape(request_batch, decode_steps, KEY_HEADS, HEAD_SIZE)
    query_rows = query_rows.reshape(request_batch, decode_steps, KEY_HEADS, QUERY_HEADS // KEY_HEADS, HEAD_SIZE)
    attention_result = attend_step(query_rows, rotated_cache_keys.reshape(request_batch, -1, KEY_HEADS, HEAD_SIZE), cached_value_rows.reshape(request_batch, -1, KEY_HEADS, HEAD_SIZE), incoming_keys, incoming_values, cached_lengths)
    output = jnp.dot(attention_result.reshape(request_batch * decode_steps, query_columns), output_weight, preferred_element_type=jnp.float32)
    return output.astype(jnp.bfloat16).reshape(request_batch, decode_steps, model_width)
```

```python
import functools
import math
import types

import jax
import jax.numpy as jnp
from jax import lax
from jax.experimental import pallas as pl
from jax.experimental.pallas import tpu as pltpu
from jax.sharding import PartitionSpec as P

QUERY_HEADS = 64
KEY_HEADS = 8
HEAD_SIZE = 128
EPSILON = 1e-05
THETA = 500000.0
MASKED = -1e30
MESH = pl.DeviceIdType.MESH
F32 = jnp.float32
BF16 = jnp.bfloat16
TP = 4
UNROLL_PEERS = 8


def each(count, body):
    if count <= UNROLL_PEERS:
        for i in range(1, count):
            body(i)
    else:

        @pl.loop(1, count)
        def _(i):
            body(i)


def dot(a, b):
    return jnp.dot(a, b, preferred_element_type=F32)


def body(n, names, *refs):
    s = types.SimpleNamespace(**dict(zip(names, refs)))
    e = lax.axis_index("ep")
    t = lax.axis_index("tp")
    rows, width = s.tok.shape
    requests = rows // 2
    half_rows = rows // 2
    feat = width // n
    half_feat = feat // 2
    slot_rows = s.b_recv.shape[1]
    part = s.b_recv.shape[2]
    q_cols = s.wq.shape[1]
    kv_cols = s.wkv.shape[1] // 2
    out_cols = s.wo.shape[1]
    half_out = out_cols // 2
    adapters = s.dn.shape[0]
    rank = s.dn.shape[2]
    kv_heads = kv_cols // HEAD_SIZE
    group = QUERY_HEADS // KEY_HEADS
    chunk = 512
    group_cols = group * HEAD_SIZE

    def up_peer(i):
        return lax.rem(e + i, n)

    def down_peer(i):
        return lax.rem(e + n - i, n)

    def tp_up(j):
        return lax.rem(t + j, TP)

    def tp_down(j):
        return lax.rem(t + TP - j, TP)

    def remote(src, dst, send, recv, ep=None, tp=None):
        return pltpu.make_async_remote_copy(
            src_ref=src,
            dst_ref=dst,
            send_sem=send,
            recv_sem=recv,
            device_id={"ep": e if ep is None else ep, "tp": t if tp is None else tp},
            device_id_type=MESH,
        )

    loads = {}
    for k, (name, src, dst) in enumerate(
        [
            ("tok", s.tok_hbm, s.tok),
            ("dn", s.dn_hbm, s.dn),
            ("wk", s.wk_hbm, s.wkv.at[:, :kv_cols]),
            ("wv", s.wv_hbm, s.wkv.at[:, kv_cols:]),
            ("wq", s.wq_hbm, s.wq),
            ("up", s.up_hbm, s.up),
            ("kc", s.kc_hbm, s.kc),
            ("vc", s.vc_hbm, s.vc),
            ("wo", s.wo_hbm, s.wo),
        ]
    ):
        loads[name] = pltpu.make_async_copy(src, dst, s.load_sem.at[k])
        loads[name].start()

    barrier = pltpu.get_barrier_semaphore()

    def greet(i):
        pl.semaphore_signal(
            barrier, inc=1, device_id={"ep": up_peer(i), "tp": t}, device_id_type=MESH
        )

    each(n, greet)
    for j in range(1, TP):
        pl.semaphore_signal(
            barrier, inc=1, device_id={"ep": e, "tp": tp_up(j)}, device_id_type=MESH
        )

    sub = lax.broadcasted_iota(jnp.int32, (rows, rows), 0)
    lane = lax.broadcasted_iota(jnp.int32, (rows, rows), 1)
    sub_req = jnp.right_shift(sub, 1)
    lane_req = jnp.right_shift(lane, 1)
    own_sub = jnp.zeros((rows, rows), jnp.int32)
    own_lane = jnp.zeros((rows, rows), jnp.int32)
    id_lane = jnp.zeros((rows, rows), jnp.int32)
    lane3 = lax.broadcasted_iota(jnp.int32, (rows, HEAD_SIZE), 0)
    position = jnp.zeros((rows, HEAD_SIZE), F32)
    for r in range(requests):
        value = s.idx_ref[r]
        owner = lax.div(value, jnp.int32(adapters))
        own_sub = jnp.where(sub_req == r, owner, own_sub)
        own_lane = jnp.where(lane_req == r, owner, own_lane)
        id_lane = jnp.where(lane_req == r, value - owner * adapters, id_lane)
        length = s.len_ref[r]
        s.lengths[r] = jnp.full((2 * group, HEAD_SIZE), length, jnp.int32)
        position = jnp.where(jnp.right_shift(lane3, 1) == r, length.astype(F32), position)
    position = position + (lane3 - 2 * jnp.right_shift(lane3, 1)).astype(F32)
    same = own_sub == own_lane
    before_lane = jnp.sum(
        jnp.where(same & (sub_req < lane_req), 1, 0), axis=0, keepdims=True
    )
    before_sub = jnp.sum(
        jnp.where(same & (lane_req < sub_req), 1, 0), axis=1, keepdims=True
    )
    slot_lane = own_lane[:1] * slot_rows + before_lane + (lane - 2 * lane_req)[:1]
    slot_sub = before_sub + (sub - 2 * sub_req)[:, :1]
    slots = n * slot_rows
    placing = (
        lax.broadcasted_iota(jnp.int32, (slots, rows), 0)
        == jnp.broadcast_to(slot_lane, (slots, rows))
    )
    label = jnp.sum(
        jnp.where(placing, jnp.broadcast_to(id_lane[:1], (slots, rows)), 0), axis=1, keepdims=True
    )
    label = jnp.broadcast_to(label, (slots, 128))
    for o in range(n):
        s.meta_send[o, :slot_rows] = label[o * slot_rows : (o + 1) * slot_rows]
        s.meta_send[o, slot_rows:] = jnp.broadcast_to(
            jnp.where(own_sub[:, :1] == o, slot_sub, -1), (rows, 128)
        )
    s.meta[e] = s.meta_send[e]

    loads["tok"].wait()
    for r in range(0, rows, 16):
        wide = s.tok[r : r + 16, :].astype(F32)
        factor = lax.rsqrt(jnp.mean(wide * wide, axis=-1, keepdims=True) + EPSILON)
        s.nrm[r : r + 16, :] = (wide * factor).astype(BF16)

    pl.semaphore_wait(barrier, n - 1 + TP - 1)

    def quarter(block, index):
        return (
            block,
            pl.ds(pl.multiple_of(lax.rem(index, 2) * half_rows, half_rows), half_rows),
            pl.ds(pl.multiple_of(lax.div(index, 2) * half_feat, 128), half_feat),
        )

    def a_copy(i):
        p = up_peer(i)
        src = s.nrm.at[
            pl.ds(pl.multiple_of(lax.rem(t, 2) * half_rows, half_rows), half_rows),
            pl.ds(pl.multiple_of(p * feat + lax.div(t, 2) * half_feat, 128), half_feat),
        ]
        return remote(src, s.x.at[quarter(e, t)], s.a_s.at[i], s.a_r.at[i], ep=p)

    each(n, lambda i: a_copy(i).start())

    def m_copy(i):
        p = up_peer(i)
        return remote(s.meta_send.at[p], s.meta.at[e], s.m_s.at[i], s.m_r.at[i], ep=p)

    each(n, lambda i: m_copy(i).start())

    own_part = s.nrm[:, pl.ds(pl.multiple_of(t * part, 128), part)]
    placed = dot(placing.astype(BF16), own_part).astype(BF16)
    s.b_send[...] = placed.reshape(n, slot_rows, part)

    def b_copy(i):
        p = up_peer(i)
        return remote(s.b_send.at[p], s.b_recv.at[e], s.b_s.at[i], s.b_r.at[i], ep=p)

    each(n, lambda i: b_copy(i).start())
    s.b_recv[e] = s.b_send[e]
    s.x[e] = s.nrm[:, pl.ds(pl.multiple_of(e * feat, 128), feat)]

    pair = lax.broadcasted_iota(jnp.int32, (rows, HEAD_SIZE), 1)
    upper = pair >= HEAD_SIZE // 2
    pair = jnp.where(upper, pair - HEAD_SIZE // 2, pair).astype(F32)
    angles = position * jnp.exp(pair * (-2.0 / HEAD_SIZE) * math.log(THETA))
    s.cos[...] = jnp.cos(angles)
    sine = jnp.sin(angles)
    s.sin[...] = jnp.where(upper, sine, -sine)

    def f_copy(i, j, index):
        block = down_peer(i)
        ref = s.x.at[quarter(block, index)]
        return remote(ref, ref, s.f_s.at[i, j], s.f_r.at[i, j], tp=tp_up(j))

    def forward(i):
        a_copy_in = remote(
            s.x.at[quarter(down_peer(i), t)],
            s.x.at[quarter(down_peer(i), t)],
            s.a_s.at[i],
            s.a_r.at[i],
            ep=up_peer(i),
        )
        a_copy_in.wait_recv()
        for j in range(1, TP):
            f_copy(i, j, t).start()

    each(n, forward)

    def b_in(i):
        m_copy(i).wait_recv()
        remote(
            s.b_send.at[up_peer(i)],
            s.b_recv.at[down_peer(i)],
            s.b_s.at[i],
            s.b_r.at[i],
            ep=up_peer(i),
        ).wait_recv()

    each(n, b_in)
    loads["dn"].wait()
    arrived = s.b_recv[...].reshape(slots, part)
    labels = s.meta[:, :slot_rows, :].reshape(slots, 128)
    total = jnp.zeros((slots, rank), F32)
    for a in range(adapters):
        total = total + jnp.where(labels[:, :rank] == a, dot(arrived, s.dn[a]), 0.0)
    s.sh_send[...] = jnp.concatenate([total, total], axis=1)

    def s_copy(j):
        return remote(s.sh_send, s.sh_recv.at[j], s.s_s.at[j], s.s_r.at[j], tp=tp_up(j))

    for j in range(1, TP):
        s_copy(j).start()

    def f_in(i):
        for j in range(1, TP):
            f_copy(i, j, tp_down(j)).wait_recv()

    each(n, f_in)
    loads["wk"].wait()
    loads["wv"].wait()
    row_block = s.x[...].reshape(n * rows, feat)

    def p_copy(i, c):
        p = up_peer(i)
        columns = pl.ds(c * chunk, chunk)
        return remote(
            s.p_send.at[p, :, columns],
            s.p_recv.at[i, :, columns],
            s.p_s.at[i, c],
            s.p_r.at[i, c],
            ep=p,
        )

    def ship(c, value):
        columns = slice(c * chunk, (c + 1) * chunk)
        s.p_wide[:, :, columns] = value.reshape(n, rows, chunk)
        s.p_send[:, :, columns] = value.astype(BF16).reshape(n, rows, chunk)
        each(n, lambda i: p_copy(i, c).start())

    q_chunks = q_cols // chunk
    kv_chunks = 2 * kv_cols // chunk
    for c in range(kv_chunks):
        ship(q_chunks + c, dot(row_block, s.wkv[:, c * chunk : (c + 1) * chunk]))

    for j in range(1, TP):
        s_copy(j).wait_recv()
        total_j = s.sh_recv[j]
        sh = s.sh_send[...] + total_j if j == 1 else sh + total_j
    sh = sh.astype(BF16)
    lane_slot = lax.broadcasted_iota(jnp.int32, (slots, 128), 1)
    offset = jnp.where(lane_slot >= rank, 1, 0)
    spread = jnp.concatenate(
        [
            jnp.where(labels == 2 * a + offset, sh, jnp.zeros_like(sh))
            for a in range(adapters // 2)
        ],
        axis=1,
    )
    loads["up"].wait()
    codes = s.meta[:, slot_rows:, :]
    blocks = lax.broadcasted_iota(jnp.int32, (n, rows, 128), 0)
    codes = jnp.where(codes >= 0, codes + blocks * slot_rows, -1).reshape(n * rows, 128)
    returning = jnp.concatenate(
        [
            jnp.where(
                codes[:, : min(128, slots)]
                == lax.broadcasted_iota(jnp.int32, (n * rows, min(128, slots)), 1) + 128 * k,
                1.0,
                0.0,
            )
            for k in range((slots + 127) // 128)
        ],
        axis=1,
    ).astype(BF16)
    up = s.up[...].reshape(adapters * rank, q_cols)
    loads["wq"].wait()
    for c in range(q_chunks):
        columns = slice(c * chunk, (c + 1) * chunk)
        delta = dot(spread, up[:, columns]).astype(BF16)
        ship(c, dot(row_block, s.wq[:, columns]) + dot(returning, delta))

    def p_sum(c):
        columns = slice(c * chunk, (c + 1) * chunk)
        each(n, lambda i: p_copy(i, c).wait_recv())
        value = s.p_wide[e, :, columns]
        for i in range(1, n):
            value = value + s.p_recv[i, :, columns].astype(F32)
        s.tot[:, columns] = value

    def rotate(value):
        return (value * s.cos[...] + pltpu.roll(value, HEAD_SIZE // 2, 1) * s.sin[...]).astype(BF16)

    for c in range(kv_chunks):
        p_sum(q_chunks + c)
    loads["kc"].wait()
    loads["vc"].wait()
    scale = 1.0 / math.sqrt(HEAD_SIZE)
    shape = (requests, 2, group, HEAD_SIZE)
    flat = (requests, 2 * group, HEAD_SIZE)
    slots_lane = lax.broadcasted_iota(jnp.int32, flat, 2)
    second = lax.broadcasted_iota(jnp.int32, (requests, 2, group, 1), 1) == 1

    def g_copy(i, g):
        columns = pl.ds(g * group_cols, group_cols)
        ref = s.att.at[e, :, columns]
        return remote(ref, ref, s.g_s.at[i, g], s.g_r.at[i, g], ep=up_peer(i))

    def attend(g):
        for c in range(g * group_cols // chunk, (g + 1) * group_cols // chunk):
            p_sum(c)
        base = q_cols + g * HEAD_SIZE
        key = rotate(s.tot[:, base : base + HEAD_SIZE]).astype(F32)
        value = s.tot[:, base + kv_cols : base + kv_cols + HEAD_SIZE].astype(BF16).astype(F32)
        for h in range(group):
            at = g * group_cols + h * HEAD_SIZE
            s.q3[:, h, :] = rotate(s.tot[:, at : at + HEAD_SIZE]).astype(F32)
            s.k3[:, h, :] = key
            s.v3[:, h, :] = value
        q = s.q3[...].reshape(shape)
        k = s.k3[...].reshape(shape)
        v = s.v3[...].reshape(shape)
        head = slice(g * HEAD_SIZE, (g + 1) * HEAD_SIZE)
        cached = lax.dot_general(
            q.reshape(flat).astype(BF16),
            s.kc[:, :, head],
            (((2,), (2,)), ((0,), (0,))),
            preferred_element_type=F32,
        )
        live = slots_lane < s.lengths[...]
        cached = jnp.where(live, cached * scale, MASKED)
        fresh0 = jnp.sum(q * k[:, 0:1], axis=-1, keepdims=True) * scale
        fresh1 = jnp.sum(q * k[:, 1:2], axis=-1, keepdims=True) * scale
        fresh1 = jnp.where(second, fresh1, MASKED)
        fresh0 = fresh0.reshape(requests, 2 * group, 1)
        fresh1 = fresh1.reshape(requests, 2 * group, 1)
        top = jnp.maximum(
            jnp.max(cached, axis=-1, keepdims=True), jnp.maximum(fresh0, fresh1)
        )
        cached = jnp.where(live, jnp.exp(cached - top), 0.0)
        fresh0 = jnp.exp(fresh0 - top)
        fresh1 = jnp.where(second.reshape(requests, 2 * group, 1), jnp.exp(fresh1 - top), 0.0)
        totals = jnp.sum(cached, axis=-1, keepdims=True) + (fresh0 + fresh1)
        mixture = lax.dot_general(
            (cached / totals).astype(BF16),
            s.vc[:, :, head],
            (((2,), (1,)), ((0,), (0,))),
            preferred_element_type=F32,
        ).reshape(shape)
        weight0 = (fresh0 / totals).astype(BF16).astype(F32).reshape(requests, 2, group, 1)
        weight1 = (fresh1 / totals).astype(BF16).astype(F32).reshape(requests, 2, group, 1)
        mixture = mixture + (weight0 * v[:, 0:1] + weight1 * v[:, 1:2])
        s.q3[...] = mixture.reshape(rows, group, HEAD_SIZE)
        for h in range(group):
            at = g * group_cols + h * HEAD_SIZE
            s.att[e, :, at : at + HEAD_SIZE] = s.q3[:, h, :].astype(BF16)
        each(n, lambda i: g_copy(i, g).start())

    for g in range(kv_heads):
        attend(g)

    b0 = lax.rem(t, 2)
    b1 = lax.div(t, 2)
    near = t + 1 - 2 * b0
    far = t + 2 - 4 * b1
    loads["wo"].wait()
    piece = min(chunk, half_out)
    pieces = half_out // piece

    def out_part(g, side, c):
        values = s.att[:, :, g * group_cols : (g + 1) * group_cols].reshape(n * rows, group_cols)
        columns = pl.ds(pl.multiple_of(side * half_out + c * piece, 128), piece)
        return dot(values, s.wo[g * group_cols : (g + 1) * group_cols, columns])

    def one_copy(c):
        columns = pl.ds(c * piece, piece)
        return remote(
            s.one_send.at[:, columns], s.one_recv.at[:, columns], s.o_s.at[c], s.o_r.at[c], tp=near
        )

    for g in range(kv_heads):
        each(n, lambda i: g_copy(i, g).wait_recv())
        for k, side in enumerate((1 - b0, b0)):
            for c in range(pieces):
                columns = slice(c * piece, (c + 1) * piece)
                value = out_part(g, side, c)
                if g > 0:
                    value = s.acc[k, :, columns] + value
                if k == 0 and g == kv_heads - 1:
                    s.one_send[:, columns] = value.astype(BF16)
                    one_copy(c).start()
                else:
                    s.acc[k, :, columns] = value

    def two_copy(c):
        columns = pl.ds(c * piece, piece)
        return remote(
            s.two_send.at[1 - b1, :, :, columns],
            s.two_recv.at[:, :, columns],
            s.t_s.at[c],
            s.t_r.at[c],
            tp=far,
        )

    for c in range(pieces):
        columns = slice(c * piece, (c + 1) * piece)
        one_copy(c).wait_recv()
        value = s.acc[1, :, columns] + s.one_recv[:, columns].astype(F32)
        value = value.reshape(n, rows, piece)
        for k in range(2):
            block = value[:, k * half_rows : (k + 1) * half_rows]
            s.two_wide[k, :, :, columns] = block
            s.two_send[k, :, :, columns] = block.astype(BF16)
        two_copy(c).start()

    def place(block, index, c):
        return (
            pl.ds(pl.multiple_of(lax.div(index, 2) * half_rows, half_rows), half_rows),
            pl.ds(
                pl.multiple_of(block * out_cols + lax.rem(index, 2) * half_out + c * piece, 128),
                piece,
            ),
        )

    def three_copy(i, c):
        p = up_peer(i)
        return remote(
            s.three_send.at[p, :, pl.ds(c * piece, piece)],
            s.out.at[place(e, t, c)],
            s.h_s.at[i, c],
            s.h_r.at[i, c],
            ep=p,
        )

    def four_copy(i, j, c, block, index):
        ref = s.out.at[place(block, index, c)]
        return remote(ref, ref, s.r_s.at[i, j, c], s.r_r.at[i, j, c], tp=tp_up(j))

    for c in range(pieces):
        columns = slice(c * piece, (c + 1) * piece)
        two_copy(c).wait_recv()
        value = s.two_wide[b1, :, :, columns] + s.two_recv[:, :, columns].astype(F32)
        s.three_send[:, :, columns] = value.astype(BF16)
        each(n, lambda i: three_copy(i, c).start())
        s.out[place(e, t, c)] = s.three_send[e, :, columns]
        for j in range(1, TP):
            four_copy(0, j, c, e, t).start()

    for c in range(pieces):

        def pass_on(i):
            ref = s.out.at[place(down_peer(i), t, c)]
            remote(ref, ref, s.h_s.at[i, c], s.h_r.at[i, c], ep=up_peer(i)).wait_recv()
            for j in range(1, TP):
                four_copy(i, j, c, down_peer(i), t).start()

        each(n, pass_on)

    def last(i):
        for c in range(pieces):
            for j in range(1, TP):
                four_copy(i, j, c, down_peer(i), tp_down(j)).wait_recv()

    last(0)
    each(n, last)
    final = pltpu.make_async_copy(s.out, s.out_hbm, s.load_sem.at[0])
    final.start()

    def drain(i):
        a_copy(i).wait_send()
        m_copy(i).wait_send()
        b_copy(i).wait_send()
        for c in range(q_chunks + kv_chunks):
            p_copy(i, c).wait_send()
        for g in range(kv_heads):
            g_copy(i, g).wait_send()
        for c in range(pieces):
            three_copy(i, c).wait_send()
            for j in range(1, TP):
                four_copy(i, j, c, down_peer(i), t).wait_send()
        for j in range(1, TP):
            f_copy(i, j, t).wait_send()

    each(n, drain)
    for j in range(1, TP):
        s_copy(j).wait_send()
        for c in range(pieces):
            four_copy(0, j, c, e, t).wait_send()
    for c in range(pieces):
        one_copy(c).wait_send()
        two_copy(c).wait_send()
    final.wait()


def local(
    tokens,
    query_weight,
    key_weight,
    value_weight,
    output_weight,
    adapter_down_maps,
    adapter_up_maps,
    rotated_cache_keys,
    cached_value_rows,
    adapter_index,
    cached_lengths,
):
    n = lax.axis_size("ep")
    requests, steps, width = tokens.shape
    rows = requests * steps
    feat, q_cols = query_weight.shape
    kv_cols = key_weight.shape[1]
    all_cols = q_cols + 2 * kv_cols
    out_cols = output_weight.shape[1]
    half_out = out_cols // 2
    part = adapter_down_maps.shape[1]
    capacity = max(2, (2 * requests + n - 1) // n)
    slot_rows = max(16, -(-capacity * steps // 16) * 16)
    slots = n * slot_rows
    group = QUERY_HEADS // KEY_HEADS
    kv_heads = kv_cols // HEAD_SIZE
    chunks = all_cols // 512
    pieces = half_out // min(512, half_out)
    vmem = pltpu.VMEM
    dma = pltpu.SemaphoreType.DMA
    scratch = dict(
        tok=vmem((rows, width), BF16),
        nrm=vmem((rows, width), BF16),
        wq=vmem(query_weight.shape, BF16),
        wkv=vmem((feat, 2 * kv_cols), BF16),
        wo=vmem(output_weight.shape, BF16),
        dn=vmem(adapter_down_maps.shape, BF16),
        up=vmem(adapter_up_maps.shape, BF16),
        kc=vmem(rotated_cache_keys.shape, BF16),
        vc=vmem(cached_value_rows.shape, BF16),
        x=vmem((n, rows, feat), BF16),
        b_send=vmem((n, slot_rows, part), BF16),
        b_recv=vmem((n, slot_rows, part), BF16),
        meta_send=vmem((n, slot_rows + rows, 128), jnp.int32),
        meta=vmem((n, slot_rows + rows, 128), jnp.int32),
        sh_send=vmem((slots, 128), F32),
        sh_recv=vmem((TP, slots, 128), F32),
        p_wide=vmem((n, rows, all_cols), F32),
        p_send=vmem((n, rows, all_cols), BF16),
        p_recv=vmem((n, rows, all_cols), BF16),
        tot=vmem((rows, all_cols), F32),
        cos=vmem((rows, HEAD_SIZE), F32),
        sin=vmem((rows, HEAD_SIZE), F32),
        lengths=vmem((requests, 2 * group, HEAD_SIZE), jnp.int32),
        q3=vmem((rows, group, HEAD_SIZE), F32),
        k3=vmem((rows, group, HEAD_SIZE), F32),
        v3=vmem((rows, group, HEAD_SIZE), F32),
        att=vmem((n, rows, q_cols), BF16),
        acc=vmem((2, n * rows, half_out), F32),
        one_send=vmem((n * rows, half_out), BF16),
        one_recv=vmem((n * rows, half_out), BF16),
        two_wide=vmem((2, n, rows // 2, half_out), F32),
        two_send=vmem((2, n, rows // 2, half_out), BF16),
        two_recv=vmem((n, rows // 2, half_out), BF16),
        three_send=vmem((n, rows // 2, half_out), BF16),
        out=vmem((rows, width), BF16),
        load_sem=dma((9,)),
        a_s=dma((n,)),
        a_r=dma((n,)),
        m_s=dma((n,)),
        m_r=dma((n,)),
        b_s=dma((n,)),
        b_r=dma((n,)),
        f_s=dma((n, TP)),
        f_r=dma((n, TP)),
        s_s=dma((TP,)),
        s_r=dma((TP,)),
        p_s=dma((n, chunks)),
        p_r=dma((n, chunks)),
        g_s=dma((n, kv_heads)),
        g_r=dma((n, kv_heads)),
        o_s=dma((pieces,)),
        o_r=dma((pieces,)),
        t_s=dma((pieces,)),
        t_r=dma((pieces,)),
        h_s=dma((n, pieces)),
        h_r=dma((n, pieces)),
        r_s=dma((n, TP, pieces)),
        r_r=dma((n, TP, pieces)),
    )
    operands = [
        "idx_ref",
        "len_ref",
        "tok_hbm",
        "wq_hbm",
        "wk_hbm",
        "wv_hbm",
        "wo_hbm",
        "dn_hbm",
        "up_hbm",
        "kc_hbm",
        "vc_hbm",
        "out_hbm",
    ]
    out = pl.pallas_call(
        functools.partial(body, n, operands + list(scratch)),
        out_shape=jax.ShapeDtypeStruct((rows, width), BF16),
        in_specs=[pl.BlockSpec(memory_space=pltpu.SMEM)] * 2
        + [pl.BlockSpec(memory_space=pl.ANY)] * 9,
        out_specs=pl.BlockSpec(memory_space=pl.ANY),
        scratch_shapes=list(scratch.values()),
        compiler_params=pltpu.CompilerParams(
            collective_id=0, has_side_effects=True, vmem_limit_bytes=60 * 2**20
        ),
        name="sublayer",
    )(
        adapter_index,
        cached_lengths,
        tokens.reshape(rows, width),
        query_weight,
        key_weight,
        value_weight,
        output_weight,
        adapter_down_maps,
        adapter_up_maps,
        rotated_cache_keys,
        cached_value_rows,
    )
    return out.reshape(tokens.shape)


def solution(mesh):
    return jax.shard_map(
        local,
        mesh=mesh,
        in_specs=(
            P(("groups", "ep"), None, None),
            P("ep", "tp"),
            P("ep", "tp"),
            P("ep", "tp"),
            P("tp", "ep"),
            P("ep", "tp", None),
            P("ep", None, "tp"),
            P(("groups", "ep"), None, "tp"),
            P(("groups", "ep"), None, "tp"),
            P(("groups", "ep")),
            P(("groups", "ep")),
        ),
        out_specs=P(("groups", "ep"), None, None),
        check_vma=False,
    )
```

```python
import functools
import math
import types

import jax
import jax.numpy as jnp
from jax import lax
from jax.experimental import pallas as pl
from jax.experimental.pallas import tpu as pltpu
from jax.sharding import PartitionSpec as P

QUERY_HEADS = 64
KEY_HEADS = 8
HEAD_SIZE = 128
EPSILON = 1e-05
THETA = 500000.0
MASKED = -1e30
MESH = pl.DeviceIdType.MESH
F32 = jnp.float32
BF16 = jnp.bfloat16
TP = 4
UNROLL_PEERS = 8


def each(count, body):
    if count <= UNROLL_PEERS:
        for i in range(1, count):
            body(i)
    else:

        @pl.loop(1, count)
        def _(i):
            body(i)


def dot(a, b):
    return jnp.dot(a, b, preferred_element_type=F32)


def body(n, names, *refs):
    s = types.SimpleNamespace(**dict(zip(names, refs)))
    e = lax.axis_index("ep")
    t = lax.axis_index("tp")
    rows, width = s.tok.shape
    requests = rows // 2
    half_rows = rows // 2
    feat = width // n
    half_feat = feat // 2
    slot_rows = s.b_recv.shape[1]
    part = s.b_recv.shape[2]
    q_cols = s.wq.shape[1]
    kv_cols = s.wkv.shape[1] // 2
    out_cols = s.wo.shape[1]
    half_out = out_cols // 2
    adapters = s.dn.shape[0]
    rank = s.dn.shape[1]
    kv_heads = kv_cols // HEAD_SIZE
    group = QUERY_HEADS // KEY_HEADS
    chunk = 512
    group_cols = group * HEAD_SIZE

    def up_peer(i):
        return lax.rem(e + i, n)

    def down_peer(i):
        return lax.rem(e + n - i, n)

    def tp_up(j):
        return lax.rem(t + j, TP)

    def tp_down(j):
        return lax.rem(t + TP - j, TP)

    def remote(src, dst, send, recv, ep=None, tp=None):
        return pltpu.make_async_remote_copy(
            src_ref=src,
            dst_ref=dst,
            send_sem=send,
            recv_sem=recv,
            device_id={"ep": e if ep is None else ep, "tp": t if tp is None else tp},
            device_id_type=MESH,
        )

    loads = {}
    for k, (name, src, dst) in enumerate(
        [
            ("tok", s.tok_hbm, s.tok),
            ("dn", s.dn_hbm, s.dn),
            ("wk", s.wk_hbm, s.wkv.at[:, :kv_cols]),
            ("wv", s.wv_hbm, s.wkv.at[:, kv_cols:]),
            ("wq", s.wq_hbm, s.wq),
            ("up", s.up_hbm, s.up),
            ("kc", s.kc_hbm, s.kc),
            ("vc", s.vc_hbm, s.vc),
            ("wo", s.wo_hbm, s.wo),
        ]
    ):
        loads[name] = pltpu.make_async_copy(src, dst, s.load_sem.at[k])
        loads[name].start()

    barrier = pltpu.get_barrier_semaphore()

    def greet(i):
        pl.semaphore_signal(
            barrier, inc=1, device_id={"ep": up_peer(i), "tp": t}, device_id_type=MESH
        )

    each(n, greet)
    for j in range(1, TP):
        pl.semaphore_signal(
            barrier, inc=1, device_id={"ep": e, "tp": tp_up(j)}, device_id_type=MESH
        )

    square = (1, rows, rows)
    sub = lax.broadcasted_iota(jnp.int32, square, 1)
    lane = lax.broadcasted_iota(jnp.int32, square, 2)
    sub_req = jnp.right_shift(sub, 1)
    lane_req = jnp.right_shift(lane, 1)
    slots = n * slot_rows

    def slots_of(flags):
        flags_sub = jnp.sum(jnp.where(sub == lane, flags, 0), axis=2, keepdims=True)
        before_lane = jnp.sum(jnp.where(sub_req < lane_req, flags_sub, 0), axis=1, keepdims=True)
        before_sub = jnp.sum(jnp.where(lane_req < sub_req, flags, 0), axis=2, keepdims=True)
        return (
            flags_sub,
            before_lane + (lane - 2 * lane_req)[:, :1],
            before_sub + (sub - 2 * sub_req)[:, :, :1],
        )

    tile_req = jnp.right_shift(lax.broadcasted_iota(jnp.int32, (8, 128), 1), 1)
    lane3 = lax.broadcasted_iota(jnp.int32, (rows, HEAD_SIZE), 0)
    position = jnp.zeros((rows, HEAD_SIZE), F32)
    own_ids = jnp.zeros((8, 128), jnp.int32)
    for r in range(requests):
        own_ids = jnp.where(tile_req == r, s.idx_ref[r], own_ids)
        length = s.len_ref[r]
        s.lengths[r] = jnp.full((2 * group, HEAD_SIZE), length, jnp.int32)
        position = jnp.where(jnp.right_shift(lane3, 1) == r, length.astype(F32), position)
    position = position + (lane3 - 2 * jnp.right_shift(lane3, 1)).astype(F32)
    s.id_send[...] = own_ids
    s.ids[e] = own_ids
    owners = lax.broadcasted_iota(jnp.int32, (n, 1, rows), 0)
    own_row = own_ids[:1, :rows].reshape(1, 1, rows) - owners * adapters
    flags = jnp.where((own_row >= 0) & (own_row < adapters), 1, 0)
    _, slot_lane, _ = slots_of(flags)
    placing = (lax.broadcasted_iota(jnp.int32, (n, slot_rows, rows), 1) == slot_lane) & (flags > 0)
    placing = jnp.where(placing, 1.0, 0.0).reshape(slots, rows)

    loads["tok"].wait()
    for r in range(0, rows, 16):
        wide = s.tok[r : r + 16, :].astype(F32)
        factor = lax.rsqrt(jnp.mean(wide * wide, axis=-1, keepdims=True) + EPSILON)
        s.nrm[r : r + 16, :] = (wide * factor).astype(BF16)

    pl.semaphore_wait(barrier, n - 1 + TP - 1)

    def quarter(block, index):
        return (
            block,
            pl.ds(pl.multiple_of(lax.rem(index, 2) * half_rows, half_rows), half_rows),
            pl.ds(pl.multiple_of(lax.div(index, 2) * half_feat, 128), half_feat),
        )

    def a_copy(i):
        p = up_peer(i)
        src = s.nrm.at[
            pl.ds(pl.multiple_of(lax.rem(t, 2) * half_rows, half_rows), half_rows),
            pl.ds(pl.multiple_of(p * feat + lax.div(t, 2) * half_feat, 128), half_feat),
        ]
        return remote(src, s.x.at[quarter(e, t)], s.a_s.at[i], s.a_r.at[i], ep=p)

    each(n, lambda i: a_copy(i).start())

    def m_copy(i):
        p = up_peer(i)
        return remote(s.id_send, s.ids.at[e], s.m_s.at[i], s.m_r.at[i], ep=p)

    each(n, lambda i: m_copy(i).start())

    own_part = s.nrm[:, pl.ds(pl.multiple_of(t * part, 128), part)]
    placed = dot(placing.astype(BF16), own_part).astype(BF16)
    s.b_send[...] = placed.reshape(n, slot_rows, part)

    def b_copy(i):
        p = up_peer(i)
        return remote(s.b_send.at[p], s.b_recv.at[e], s.b_s.at[i], s.b_r.at[i], ep=p)

    each(n, lambda i: b_copy(i).start())
    s.b_recv[e] = s.b_send[e]
    s.x[e] = s.nrm[:, pl.ds(pl.multiple_of(e * feat, 128), feat)]

    pair = lax.broadcasted_iota(jnp.int32, (rows, HEAD_SIZE), 1)
    upper = pair >= HEAD_SIZE // 2
    pair = jnp.where(upper, pair - HEAD_SIZE // 2, pair).astype(F32)
    angles = position * jnp.exp(pair * (-2.0 / HEAD_SIZE) * math.log(THETA))
    s.cos[...] = jnp.cos(angles)
    sine = jnp.sin(angles)
    s.sin[...] = jnp.where(upper, sine, -sine)

    b0 = lax.rem(t, 2)
    b1 = lax.div(t, 2)
    near = t + 1 - 2 * b0
    far = t + 2 - 4 * b1
    across = near + 2 - 4 * b1

    def f_copy(i, k, index):
        ref = s.x.at[quarter(down_peer(i), index)]
        return remote(ref, ref, s.f_s.at[i, k], s.f_r.at[i, k], tp=far if k == 1 else near)

    def forward(i):
        ref = s.x.at[quarter(down_peer(i), t)]
        remote(ref, ref, s.a_s.at[i], s.a_r.at[i], ep=up_peer(i)).wait_recv()
        f_copy(i, 1, t).start()
        f_copy(i, 0, t).start()

    def forward_far(i):
        f_copy(i, 1, far).wait_recv()
        f_copy(i, 2, far).start()

    each(n, forward)
    each(n, forward_far)

    def b_in(i):
        m_copy(i).wait_recv()
        remote(
            s.b_send.at[up_peer(i)],
            s.b_recv.at[down_peer(i)],
            s.b_s.at[i],
            s.b_r.at[i],
            ep=up_peer(i),
        ).wait_recv()

    each(n, b_in)
    loads["dn"].wait()
    arrived = s.b_recv[...].reshape(slots, part)
    ids = s.ids[:, :1, :rows] - e * adapters
    flags = jnp.where((ids >= 0) & (ids < adapters), 1, 0)
    flags_sub, slot_lane, slot_sub = slots_of(flags)
    taken = (lax.broadcasted_iota(jnp.int32, (n, slot_rows, rows), 1) == slot_lane) & (flags > 0)
    labels = jnp.sum(jnp.where(taken, ids, 0), axis=2, keepdims=True)
    labels = jnp.broadcast_to(labels, (n, slot_rows, 128)).reshape(slots, 128)
    lane_slot = lax.broadcasted_iota(jnp.int32, (slots, 128), 1)
    offset = jnp.where(lane_slot >= rank, 1, 0)
    down = lax.dot_general(
        arrived,
        s.dn[...].reshape(adapters * rank, part),
        (((1,), (1,)), ((), ())),
        preferred_element_type=F32,
    )
    total = jnp.zeros((slots, 128), F32)
    for a in range(adapters // 2):
        block = down[:, 128 * a : 128 * (a + 1)]
        total = total + jnp.where(labels == 2 * a + offset, block, 0.0)
    s.sh_send[...] = total + pltpu.roll(total, rank, 1)

    def s_copy(j):
        return remote(s.sh_send, s.sh_recv.at[j], s.s_s.at[j], s.s_r.at[j], tp=tp_up(j))

    for j in range(1, TP):
        s_copy(j).start()

    def f_in(i):
        f_copy(i, 0, near).wait_recv()
        f_copy(i, 2, across).wait_recv()

    each(n, f_in)
    loads["wk"].wait()
    loads["wv"].wait()
    row_block = s.x[...].reshape(n * rows, feat)

    def p_copy(i, c):
        p = up_peer(i)
        columns = pl.ds(c * chunk, chunk)
        return remote(
            s.p_send.at[p, :, columns],
            s.p_recv.at[i, :, columns],
            s.p_s.at[i, c],
            s.p_r.at[i, c],
            ep=p,
        )

    def ship(c, value):
        columns = slice(c * chunk, (c + 1) * chunk)
        s.p_wide[:, :, columns] = value.reshape(n, rows, chunk)
        s.p_send[:, :, columns] = value.astype(BF16).reshape(n, rows, chunk)
        each(n, lambda i: p_copy(i, c).start())

    q_chunks = q_cols // chunk
    kv_chunks = 2 * kv_cols // chunk
    for c in range(kv_chunks):
        ship(q_chunks + c, dot(row_block, s.wkv[:, c * chunk : (c + 1) * chunk]))

    for j in range(1, TP):
        s_copy(j).wait_recv()
        total_j = s.sh_recv[j]
        sh = s.sh_send[...] + total_j if j == 1 else sh + total_j
    sh = sh.astype(BF16)
    spread = jnp.concatenate(
        [
            jnp.where(labels == 2 * a + offset, sh, jnp.zeros_like(sh))
            for a in range(adapters // 2)
        ],
        axis=1,
    )
    loads["up"].wait()
    block = lax.broadcasted_iota(jnp.int32, (n, rows, 1), 0) * slot_rows
    codes = jnp.where(flags_sub > 0, slot_sub + block, -1)
    returning = lax.broadcasted_iota(jnp.int32, (n, rows, slots), 2) == codes
    returning = jnp.where(returning, 1.0, 0.0).reshape(n * rows, slots).astype(BF16)
    up = s.up[...].reshape(adapters * rank, q_cols)
    loads["wq"].wait()
    for c in range(q_chunks):
        columns = slice(c * chunk, (c + 1) * chunk)
        delta = dot(spread, up[:, columns]).astype(BF16)
        ship(c, dot(row_block, s.wq[:, columns]) + dot(returning, delta))

    def p_sum(c):
        columns = slice(c * chunk, (c + 1) * chunk)
        each(n, lambda i: p_copy(i, c).wait_recv())
        value = s.p_wide[e, :, columns]
        for i in range(1, n):
            value = value + s.p_recv[i, :, columns].astype(F32)
        s.tot[:, columns] = value

    def rotate(value):
        return (value * s.cos[...] + pltpu.roll(value, HEAD_SIZE // 2, 1) * s.sin[...]).astype(BF16)

    for c in range(kv_chunks):
        p_sum(q_chunks + c)
    loads["kc"].wait()
    loads["vc"].wait()
    scale = 1.0 / math.sqrt(HEAD_SIZE)
    shape = (requests, 2, group, HEAD_SIZE)
    flat = (requests, 2 * group, HEAD_SIZE)
    slots_lane = lax.broadcasted_iota(jnp.int32, flat, 2)
    second = lax.broadcasted_iota(jnp.int32, (requests, 2, group, 1), 1) == 1

    def g_copy(i, g):
        columns = pl.ds(g * group_cols, group_cols)
        ref = s.att.at[e, :, columns]
        return remote(ref, ref, s.g_s.at[i, g], s.g_r.at[i, g], ep=up_peer(i))

    def attend(g):
        for c in range(g * group_cols // chunk, (g + 1) * group_cols // chunk):
            p_sum(c)
        base = q_cols + g * HEAD_SIZE
        key = rotate(s.tot[:, base : base + HEAD_SIZE]).astype(F32)
        value = s.tot[:, base + kv_cols : base + kv_cols + HEAD_SIZE].astype(BF16).astype(F32)
        for h in range(group):
            at = g * group_cols + h * HEAD_SIZE
            s.q3[:, h, :] = rotate(s.tot[:, at : at + HEAD_SIZE]).astype(F32)
            s.k3[:, h, :] = key
            s.v3[:, h, :] = value
        q = s.q3[...].reshape(shape)
        k = s.k3[...].reshape(shape)
        v = s.v3[...].reshape(shape)
        head = slice(g * HEAD_SIZE, (g + 1) * HEAD_SIZE)
        cached = lax.dot_general(
            q.reshape(flat).astype(BF16),
            s.kc[:, :, head],
            (((2,), (2,)), ((0,), (0,))),
            preferred_element_type=F32,
        )
        live = slots_lane < s.lengths[...]
        cached = jnp.where(live, cached * scale, MASKED)
        fresh0 = jnp.sum(q * k[:, 0:1], axis=-1, keepdims=True) * scale
        fresh1 = jnp.sum(q * k[:, 1:2], axis=-1, keepdims=True) * scale
        fresh1 = jnp.where(second, fresh1, MASKED)
        fresh0 = fresh0.reshape(requests, 2 * group, 1)
        fresh1 = fresh1.reshape(requests, 2 * group, 1)
        top = jnp.maximum(
            jnp.max(cached, axis=-1, keepdims=True), jnp.maximum(fresh0, fresh1)
        )
        cached = jnp.where(live, jnp.exp(cached - top), 0.0)
        fresh0 = jnp.exp(fresh0 - top)
        fresh1 = jnp.where(second.reshape(requests, 2 * group, 1), jnp.exp(fresh1 - top), 0.0)
        totals = jnp.sum(cached, axis=-1, keepdims=True) + (fresh0 + fresh1)
        mixture = lax.dot_general(
            (cached / totals).astype(BF16),
            s.vc[:, :, head],
            (((2,), (1,)), ((0,), (0,))),
            preferred_element_type=F32,
        ).reshape(shape)
        weight0 = (fresh0 / totals).astype(BF16).astype(F32).reshape(requests, 2, group, 1)
        weight1 = (fresh1 / totals).astype(BF16).astype(F32).reshape(requests, 2, group, 1)
        mixture = mixture + (weight0 * v[:, 0:1] + weight1 * v[:, 1:2])
        s.q3[...] = mixture.reshape(rows, group, HEAD_SIZE)
        for h in range(group):
            at = g * group_cols + h * HEAD_SIZE
            s.att[e, :, at : at + HEAD_SIZE] = s.q3[:, h, :].astype(BF16)
        each(n, lambda i: g_copy(i, g).start())

    for g in range(kv_heads):
        attend(g)

    loads["wo"].wait()
    piece = min(chunk, half_out)
    pieces = half_out // piece

    def out_part(g, side, c):
        values = s.att[:, :, g * group_cols : (g + 1) * group_cols].reshape(n * rows, group_cols)
        columns = pl.ds(pl.multiple_of(side * half_out + c * piece, 128), piece)
        return dot(values, s.wo[g * group_cols : (g + 1) * group_cols, columns])

    def one_copy(c):
        columns = pl.ds(c * piece, piece)
        return remote(
            s.one_send.at[:, columns], s.one_recv.at[:, columns], s.o_s.at[c], s.o_r.at[c], tp=near
        )

    for g in range(kv_heads):
        each(n, lambda i: g_copy(i, g).wait_recv())
        for k, side in enumerate((1 - b0, b0)):
            for c in range(pieces):
                columns = slice(c * piece, (c + 1) * piece)
                value = out_part(g, side, c)
                if g > 0:
                    value = s.acc[k, :, columns] + value
                if k == 0 and g == kv_heads - 1:
                    s.one_send[:, columns] = value.astype(BF16)
                    one_copy(c).start()
                else:
                    s.acc[k, :, columns] = value

    def two_copy(c):
        columns = pl.ds(c * piece, piece)
        return remote(
            s.two_send.at[1 - b1, :, :, columns],
            s.two_recv.at[:, :, columns],
            s.t_s.at[c],
            s.t_r.at[c],
            tp=far,
        )

    for c in range(pieces):
        columns = slice(c * piece, (c + 1) * piece)
        one_copy(c).wait_recv()
        value = s.acc[1, :, columns] + s.one_recv[:, columns].astype(F32)
        value = value.reshape(n, rows, piece)
        for k in range(2):
            block = value[:, k * half_rows : (k + 1) * half_rows]
            s.two_wide[k, :, :, columns] = block
            s.two_send[k, :, :, columns] = block.astype(BF16)
        two_copy(c).start()

    def place(block, index, c):
        return (
            pl.ds(pl.multiple_of(lax.div(index, 2) * half_rows, half_rows), half_rows),
            pl.ds(
                pl.multiple_of(block * out_cols + lax.rem(index, 2) * half_out + c * piece, 128),
                piece,
            ),
        )

    def three_copy(i, c):
        p = up_peer(i)
        return remote(
            s.three_send.at[p, :, pl.ds(c * piece, piece)],
            s.out.at[place(e, t, c)],
            s.h_s.at[i, c],
            s.h_r.at[i, c],
            ep=p,
        )

    def four_copy(i, k, c, index):
        ref = s.out.at[place(down_peer(i), index, c)]
        return remote(
            ref, ref, s.r_s.at[i, k, c], s.r_r.at[i, k, c], tp=far if k == 1 else near
        )

    def pass_far(i, c):
        four_copy(i, 1, c, far).wait_recv()
        four_copy(i, 2, c, far).start()

    for c in range(pieces):
        columns = slice(c * piece, (c + 1) * piece)
        two_copy(c).wait_recv()
        value = s.two_wide[b1, :, :, columns] + s.two_recv[:, :, columns].astype(F32)
        s.three_send[:, :, columns] = value.astype(BF16)
        each(n, lambda i: three_copy(i, c).start())
        s.out[place(e, t, c)] = s.three_send[e, :, columns]
        four_copy(0, 1, c, t).start()
        four_copy(0, 0, c, t).start()

    for c in range(pieces):

        def pass_on(i):
            ref = s.out.at[place(down_peer(i), t, c)]
            remote(ref, ref, s.h_s.at[i, c], s.h_r.at[i, c], ep=up_peer(i)).wait_recv()
            four_copy(i, 1, c, t).start()
            four_copy(i, 0, c, t).start()

        pass_far(0, c)
        each(n, pass_on)
        each(n, lambda i: pass_far(i, c))

    def last(i):
        for c in range(pieces):
            four_copy(i, 0, c, near).wait_recv()
            four_copy(i, 2, c, across).wait_recv()

    last(0)
    each(n, last)
    final = pltpu.make_async_copy(s.out, s.out_hbm, s.load_sem.at[0])
    final.start()

    def drain(i):
        a_copy(i).wait_send()
        m_copy(i).wait_send()
        b_copy(i).wait_send()
        for c in range(q_chunks + kv_chunks):
            p_copy(i, c).wait_send()
        for g in range(kv_heads):
            g_copy(i, g).wait_send()
        for c in range(pieces):
            three_copy(i, c).wait_send()
            for k in range(3):
                four_copy(i, k, c, t).wait_send()
        for k in range(3):
            f_copy(i, k, t).wait_send()

    each(n, drain)
    for j in range(1, TP):
        s_copy(j).wait_send()
    for c in range(pieces):
        for k in range(3):
            four_copy(0, k, c, t).wait_send()
        one_copy(c).wait_send()
        two_copy(c).wait_send()
    final.wait()


def local(
    tokens,
    query_weight,
    key_weight,
    value_weight,
    output_weight,
    adapter_down_maps,
    adapter_up_maps,
    rotated_cache_keys,
    cached_value_rows,
    adapter_index,
    cached_lengths,
):
    n = lax.axis_size("ep")
    requests, steps, width = tokens.shape
    rows = requests * steps
    feat, q_cols = query_weight.shape
    kv_cols = key_weight.shape[1]
    all_cols = q_cols + 2 * kv_cols
    out_cols = output_weight.shape[1]
    half_out = out_cols // 2
    adapters, part, rank = adapter_down_maps.shape
    capacity = max(2, (2 * requests + n - 1) // n)
    slot_rows = max(16, -(-capacity * steps // 16) * 16)
    slots = n * slot_rows
    group = QUERY_HEADS // KEY_HEADS
    kv_heads = kv_cols // HEAD_SIZE
    chunks = all_cols // 512
    pieces = half_out // min(512, half_out)
    vmem = pltpu.VMEM
    dma = pltpu.SemaphoreType.DMA
    scratch = dict(
        tok=vmem((rows, width), BF16),
        nrm=vmem((rows, width), BF16),
        wq=vmem(query_weight.shape, BF16),
        wkv=vmem((feat, 2 * kv_cols), BF16),
        wo=vmem(output_weight.shape, BF16),
        dn=vmem((adapters, rank, part), BF16),
        up=vmem(adapter_up_maps.shape, BF16),
        kc=vmem(rotated_cache_keys.shape, BF16),
        vc=vmem(cached_value_rows.shape, BF16),
        x=vmem((n, rows, feat), BF16),
        b_send=vmem((n, slot_rows, part), BF16),
        b_recv=vmem((n, slot_rows, part), BF16),
        id_send=vmem((8, 128), jnp.int32),
        ids=vmem((n, 8, 128), jnp.int32),
        sh_send=vmem((slots, 128), F32),
        sh_recv=vmem((TP, slots, 128), F32),
        p_wide=vmem((n, rows, all_cols), F32),
        p_send=vmem((n, rows, all_cols), BF16),
        p_recv=vmem((n, rows, all_cols), BF16),
        tot=vmem((rows, all_cols), F32),
        cos=vmem((rows, HEAD_SIZE), F32),
        sin=vmem((rows, HEAD_SIZE), F32),
        lengths=vmem((requests, 2 * group, HEAD_SIZE), jnp.int32),
        q3=vmem((rows, group, HEAD_SIZE), F32),
        k3=vmem((rows, group, HEAD_SIZE), F32),
        v3=vmem((rows, group, HEAD_SIZE), F32),
        att=vmem((n, rows, q_cols), BF16),
        acc=vmem((2, n * rows, half_out), F32),
        one_send=vmem((n * rows, half_out), BF16),
        one_recv=vmem((n * rows, half_out), BF16),
        two_wide=vmem((2, n, rows // 2, half_out), F32),
        two_send=vmem((2, n, rows // 2, half_out), BF16),
        two_recv=vmem((n, rows // 2, half_out), BF16),
        three_send=vmem((n, rows // 2, half_out), BF16),
        out=vmem((rows, width), BF16),
        load_sem=dma((9,)),
        a_s=dma((n,)),
        a_r=dma((n,)),
        m_s=dma((n,)),
        m_r=dma((n,)),
        b_s=dma((n,)),
        b_r=dma((n,)),
        f_s=dma((n, TP)),
        f_r=dma((n, TP)),
        s_s=dma((TP,)),
        s_r=dma((TP,)),
        p_s=dma((n, chunks)),
        p_r=dma((n, chunks)),
        g_s=dma((n, kv_heads)),
        g_r=dma((n, kv_heads)),
        o_s=dma((pieces,)),
        o_r=dma((pieces,)),
        t_s=dma((pieces,)),
        t_r=dma((pieces,)),
        h_s=dma((n, pieces)),
        h_r=dma((n, pieces)),
        r_s=dma((n, TP, pieces)),
        r_r=dma((n, TP, pieces)),
    )
    operands = [
        "idx_ref",
        "len_ref",
        "tok_hbm",
        "wq_hbm",
        "wk_hbm",
        "wv_hbm",
        "wo_hbm",
        "dn_hbm",
        "up_hbm",
        "kc_hbm",
        "vc_hbm",
        "out_hbm",
    ]
    out = pl.pallas_call(
        functools.partial(body, n, operands + list(scratch)),
        out_shape=jax.ShapeDtypeStruct((rows, width), BF16),
        in_specs=[pl.BlockSpec(memory_space=pltpu.SMEM)] * 2
        + [pl.BlockSpec(memory_space=pl.ANY)] * 9,
        out_specs=pl.BlockSpec(memory_space=pl.ANY),
        scratch_shapes=list(scratch.values()),
        compiler_params=pltpu.CompilerParams(
            collective_id=0, has_side_effects=True, vmem_limit_bytes=60 * 2**20
        ),
        name="sublayer",
    )(
        adapter_index,
        cached_lengths,
        tokens.reshape(rows, width),
        query_weight,
        key_weight,
        value_weight,
        output_weight,
        jnp.swapaxes(adapter_down_maps, 1, 2),
        adapter_up_maps,
        rotated_cache_keys,
        cached_value_rows,
    )
    return out.reshape(tokens.shape)


def solution(mesh):
    return jax.shard_map(
        local,
        mesh=mesh,
        in_specs=(
            P(("groups", "ep"), None, None),
            P("ep", "tp"),
            P("ep", "tp"),
            P("ep", "tp"),
            P("tp", "ep"),
            P("ep", "tp", None),
            P("ep", None, "tp"),
            P(("groups", "ep"), None, "tp"),
            P(("groups", "ep"), None, "tp"),
            P(("groups", "ep")),
            P(("groups", "ep")),
        ),
        out_specs=P(("groups", "ep"), None, None),
        check_vma=False,
    )
```

```python
import functools
import math
import types

import jax
import jax.numpy as jnp
from jax import lax
from jax.experimental import pallas as pl
from jax.experimental.pallas import tpu as pltpu
from jax.sharding import PartitionSpec as P

QUERY_HEADS = 64
KEY_HEADS = 8
HEAD_SIZE = 128
EPSILON = 1e-05
THETA = 500000.0
MASKED = -1e30
MESH = pl.DeviceIdType.MESH
F32 = jnp.float32
BF16 = jnp.bfloat16
TP = 4
UNROLL_PEERS = 8


def each(count, body):
    if count <= UNROLL_PEERS:
        for i in range(1, count):
            body(i)
    else:

        @pl.loop(1, count)
        def _(i):
            body(i)


def dot(a, b):
    return jnp.dot(a, b, preferred_element_type=F32)


def body(n, names, *refs):
    s = types.SimpleNamespace(**dict(zip(names, refs)))
    e = lax.axis_index("ep")
    t = lax.axis_index("tp")
    rows, width = s.tok.shape
    requests = rows // 2
    half_rows = rows // 2
    feat = width // n
    half_feat = feat // 2
    slot_rows = s.b_recv.shape[1]
    part = s.b_recv.shape[2]
    q_cols = s.wq.shape[1]
    kv_cols = s.wkv.shape[1] // 2
    out_cols = s.wo.shape[1]
    half_out = out_cols // 2
    adapters = s.dn.shape[0]
    rank = s.dn.shape[1]
    kv_heads = kv_cols // HEAD_SIZE
    group = QUERY_HEADS // KEY_HEADS
    chunk = 512
    group_cols = group * HEAD_SIZE

    def partner(i):
        both = 0
        bit = 1
        while bit < n:
            both = both + bit * (lax.rem(lax.div(e, bit), 2) * ((i // bit) % 2))
            bit *= 2
        return e + i - 2 * both

    def tp_up(j):
        return lax.rem(t + j, TP)

    def tp_down(j):
        return lax.rem(t + TP - j, TP)

    def remote(src, dst, send, recv, ep=None, tp=None):
        return pltpu.make_async_remote_copy(
            src_ref=src,
            dst_ref=dst,
            send_sem=send,
            recv_sem=recv,
            device_id={"ep": e if ep is None else ep, "tp": t if tp is None else tp},
            device_id_type=MESH,
        )

    loads = {}
    for k, (name, src, dst) in enumerate(
        [
            ("tok", s.tok_hbm, s.tok),
            ("dn", s.dn_hbm, s.dn),
            ("wk", s.wk_hbm, s.wkv.at[:, :kv_cols]),
            ("wv", s.wv_hbm, s.wkv.at[:, kv_cols:]),
            ("wq", s.wq_hbm, s.wq),
            ("up", s.up_hbm, s.up),
            ("kc", s.kc_hbm, s.kc),
            ("vc", s.vc_hbm, s.vc),
            ("wo", s.wo_hbm, s.wo),
        ]
    ):
        loads[name] = pltpu.make_async_copy(src, dst, s.load_sem.at[k])
        loads[name].start()

    barrier = pltpu.get_barrier_semaphore()

    def greet(i):
        pl.semaphore_signal(
            barrier, inc=1, device_id={"ep": partner(i), "tp": t}, device_id_type=MESH
        )

    each(n, greet)
    for j in range(1, TP):
        pl.semaphore_signal(
            barrier, inc=1, device_id={"ep": e, "tp": tp_up(j)}, device_id_type=MESH
        )

    square = (1, rows, rows)
    sub = lax.broadcasted_iota(jnp.int32, square, 1)
    lane = lax.broadcasted_iota(jnp.int32, square, 2)
    sub_req = jnp.right_shift(sub, 1)
    lane_req = jnp.right_shift(lane, 1)
    slots = n * slot_rows

    def slots_of(flags):
        flags_sub = jnp.sum(jnp.where(sub == lane, flags, 0), axis=2, keepdims=True)
        before_lane = jnp.sum(jnp.where(sub_req < lane_req, flags_sub, 0), axis=1, keepdims=True)
        before_sub = jnp.sum(jnp.where(lane_req < sub_req, flags, 0), axis=2, keepdims=True)
        return (
            flags_sub,
            before_lane + (lane - 2 * lane_req)[:, :1],
            before_sub + (sub - 2 * sub_req)[:, :, :1],
        )

    tile_req = jnp.right_shift(lax.broadcasted_iota(jnp.int32, (8, 128), 1), 1)
    lane3 = lax.broadcasted_iota(jnp.int32, (rows, HEAD_SIZE), 0)
    position = jnp.zeros((rows, HEAD_SIZE), F32)
    own_ids = jnp.zeros((8, 128), jnp.int32)
    for r in range(requests):
        own_ids = jnp.where(tile_req == r, s.idx_ref[r], own_ids)
        length = s.len_ref[r]
        s.lengths[r] = jnp.full((2 * group, HEAD_SIZE), length, jnp.int32)
        position = jnp.where(jnp.right_shift(lane3, 1) == r, length.astype(F32), position)
    position = position + (lane3 - 2 * jnp.right_shift(lane3, 1)).astype(F32)
    s.id_send[...] = own_ids
    s.ids[e] = own_ids
    owners = lax.broadcasted_iota(jnp.int32, (n, 1, rows), 0)
    own_row = own_ids[:1, :rows].reshape(1, 1, rows) - owners * adapters
    flags = jnp.where((own_row >= 0) & (own_row < adapters), 1, 0)
    _, slot_lane, _ = slots_of(flags)
    placing = (lax.broadcasted_iota(jnp.int32, (n, slot_rows, rows), 1) == slot_lane) & (flags > 0)
    placing = jnp.where(placing, 1.0, 0.0).reshape(slots, rows)

    loads["tok"].wait()
    for r in range(0, rows, 16):
        wide = s.tok[r : r + 16, :].astype(F32)
        factor = lax.rsqrt(jnp.mean(wide * wide, axis=-1, keepdims=True) + EPSILON)
        s.nrm[r : r + 16, :] = (wide * factor).astype(BF16)

    pl.semaphore_wait(barrier, n - 1 + TP - 1)

    def quarter(block, index):
        return (
            block,
            pl.ds(pl.multiple_of(lax.rem(index, 2) * half_rows, half_rows), half_rows),
            pl.ds(pl.multiple_of(lax.div(index, 2) * half_feat, 128), half_feat),
        )

    def a_copy(i):
        p = partner(i)
        src = s.nrm.at[
            pl.ds(pl.multiple_of(lax.rem(t, 2) * half_rows, half_rows), half_rows),
            pl.ds(pl.multiple_of(p * feat + lax.div(t, 2) * half_feat, 128), half_feat),
        ]
        return remote(src, s.x.at[quarter(e, t)], s.a_s.at[i], s.a_r.at[i], ep=p)

    each(n, lambda i: a_copy(i).start())

    def m_copy(i):
        p = partner(i)
        return remote(s.id_send, s.ids.at[e], s.m_s.at[i], s.m_r.at[i], ep=p)

    each(n, lambda i: m_copy(i).start())

    own_part = s.nrm[:, pl.ds(pl.multiple_of(t * part, 128), part)]
    placed = dot(placing.astype(BF16), own_part).astype(BF16)
    s.b_send[...] = placed.reshape(n, slot_rows, part)

    def b_copy(i):
        p = partner(i)
        return remote(s.b_send.at[p], s.b_recv.at[e], s.b_s.at[i], s.b_r.at[i], ep=p)

    each(n, lambda i: b_copy(i).start())
    s.b_recv[e] = s.b_send[e]
    s.x[e] = s.nrm[:, pl.ds(pl.multiple_of(e * feat, 128), feat)]

    pair = lax.broadcasted_iota(jnp.int32, (rows, HEAD_SIZE), 1)
    upper = pair >= HEAD_SIZE // 2
    pair = jnp.where(upper, pair - HEAD_SIZE // 2, pair).astype(F32)
    angles = position * jnp.exp(pair * (-2.0 / HEAD_SIZE) * math.log(THETA))
    s.cos[...] = jnp.cos(angles)
    sine = jnp.sin(angles)
    s.sin[...] = jnp.where(upper, sine, -sine)

    b0 = lax.rem(t, 2)
    b1 = lax.div(t, 2)
    near = t + 1 - 2 * b0
    far = t + 2 - 4 * b1
    across = near + 2 - 4 * b1

    def f_copy(i, k, index):
        ref = s.x.at[quarter(partner(i), index)]
        return remote(ref, ref, s.f_s.at[i, k], s.f_r.at[i, k], tp=far if k == 1 else near)

    def forward(i):
        ref = s.x.at[quarter(partner(i), t)]
        remote(ref, ref, s.a_s.at[i], s.a_r.at[i], ep=partner(i)).wait_recv()
        f_copy(i, 1, t).start()
        f_copy(i, 0, t).start()

    def forward_far(i):
        f_copy(i, 1, far).wait_recv()
        f_copy(i, 2, far).start()

    each(n, forward)
    each(n, forward_far)

    def b_in(i):
        m_copy(i).wait_recv()
        remote(
            s.b_send.at[partner(i)],
            s.b_recv.at[partner(i)],
            s.b_s.at[i],
            s.b_r.at[i],
            ep=partner(i),
        ).wait_recv()

    each(n, b_in)
    loads["dn"].wait()
    arrived = s.b_recv[...].reshape(slots, part)
    ids = s.ids[:, :1, :rows] - e * adapters
    flags = jnp.where((ids >= 0) & (ids < adapters), 1, 0)
    flags_sub, slot_lane, slot_sub = slots_of(flags)
    taken = (lax.broadcasted_iota(jnp.int32, (n, slot_rows, rows), 1) == slot_lane) & (flags > 0)
    labels = jnp.sum(jnp.where(taken, ids, 0), axis=2, keepdims=True)
    labels = jnp.broadcast_to(labels, (n, slot_rows, 128)).reshape(slots, 128)
    lane_slot = lax.broadcasted_iota(jnp.int32, (slots, 128), 1)
    offset = jnp.where(lane_slot >= rank, 1, 0)
    down = lax.dot_general(
        arrived,
        s.dn[...].reshape(adapters * rank, part),
        (((1,), (1,)), ((), ())),
        preferred_element_type=F32,
    )
    total = jnp.zeros((slots, 128), F32)
    for a in range(adapters // 2):
        block = down[:, 128 * a : 128 * (a + 1)]
        total = total + jnp.where(labels == 2 * a + offset, block, 0.0)
    s.sh_send[...] = total + pltpu.roll(total, rank, 1)

    def s_copy(j):
        return remote(s.sh_send, s.sh_recv.at[j], s.s_s.at[j], s.s_r.at[j], tp=tp_up(j))

    for j in range(1, TP):
        s_copy(j).start()

    def f_in(i):
        f_copy(i, 0, near).wait_recv()
        f_copy(i, 2, across).wait_recv()

    each(n, f_in)
    loads["wk"].wait()
    loads["wv"].wait()
    row_block = s.x[...].reshape(n * rows, feat)

    def p_copy(i, c):
        p = partner(i)
        columns = pl.ds(c * chunk, chunk)
        return remote(
            s.p_send.at[p, :, columns],
            s.p_recv.at[i, :, columns],
            s.p_s.at[i, c],
            s.p_r.at[i, c],
            ep=p,
        )

    def ship(c, value):
        columns = slice(c * chunk, (c + 1) * chunk)
        s.p_wide[:, columns] = value
        s.p_send[:, :, columns] = value.astype(BF16).reshape(n, rows, chunk)
        each(n, lambda i: p_copy(i, c).start())

    q_chunks = q_cols // chunk
    kv_chunks = 2 * kv_cols // chunk
    for c in range(kv_chunks):
        ship(q_chunks + c, dot(row_block, s.wkv[:, c * chunk : (c + 1) * chunk]))

    loads["wq"].wait()
    for c in range(q_chunks):
        columns = slice(c * chunk, (c + 1) * chunk)
        s.p_wide[:, columns] = dot(row_block, s.wq[:, columns])

    for j in range(1, TP):
        s_copy(j).wait_recv()
        total_j = s.sh_recv[j]
        sh = s.sh_send[...] + total_j if j == 1 else sh + total_j
    sh = sh.astype(BF16)
    spread = jnp.concatenate(
        [
            jnp.where(labels == 2 * a + offset, sh, jnp.zeros_like(sh))
            for a in range(adapters // 2)
        ],
        axis=1,
    )
    loads["up"].wait()
    block = lax.broadcasted_iota(jnp.int32, (n, rows, 1), 0) * slot_rows
    codes = jnp.where(flags_sub > 0, slot_sub + block, -1)
    returning = lax.broadcasted_iota(jnp.int32, (n, rows, slots), 2) == codes
    returning = jnp.where(returning, 1.0, 0.0).reshape(n * rows, slots).astype(BF16)
    up = s.up[...].reshape(adapters * rank, q_cols)
    for c in range(q_chunks):
        columns = slice(c * chunk, (c + 1) * chunk)
        delta = dot(spread, up[:, columns]).astype(BF16)
        ship(c, s.p_wide[:, columns] + dot(returning, delta))

    def p_sum(c):
        columns = slice(c * chunk, (c + 1) * chunk)
        each(n, lambda i: p_copy(i, c).wait_recv())
        value = s.p_wide[pl.ds(pl.multiple_of(e * rows, rows), rows), columns]
        for i in range(1, n):
            value = value + s.p_recv[i, :, columns].astype(F32)
        s.tot[:, columns] = value

    def rotate(value):
        return (value * s.cos[...] + pltpu.roll(value, HEAD_SIZE // 2, 1) * s.sin[...]).astype(BF16)

    for c in range(kv_chunks):
        p_sum(q_chunks + c)
    loads["kc"].wait()
    loads["vc"].wait()
    scale = 1.0 / math.sqrt(HEAD_SIZE)
    shape = (requests, 2, group, HEAD_SIZE)
    flat = (requests, 2 * group, HEAD_SIZE)
    slots_lane = lax.broadcasted_iota(jnp.int32, flat, 2)
    second = lax.broadcasted_iota(jnp.int32, (requests, 2, group, 1), 1) == 1

    def g_copy(i, g):
        columns = pl.ds(g * group_cols, group_cols)
        ref = s.att.at[e, :, columns]
        return remote(ref, ref, s.g_s.at[i, g], s.g_r.at[i, g], ep=partner(i))

    def attend(g):
        for c in range(g * group_cols // chunk, (g + 1) * group_cols // chunk):
            p_sum(c)
        base = q_cols + g * HEAD_SIZE
        key = rotate(s.tot[:, base : base + HEAD_SIZE]).astype(F32)
        value = s.tot[:, base + kv_cols : base + kv_cols + HEAD_SIZE].astype(BF16).astype(F32)
        for h in range(group):
            at = g * group_cols + h * HEAD_SIZE
            s.q3[:, h, :] = rotate(s.tot[:, at : at + HEAD_SIZE]).astype(F32)
            s.k3[:, h, :] = key
            s.v3[:, h, :] = value
        q = s.q3[...].reshape(shape)
        k = s.k3[...].reshape(shape)
        v = s.v3[...].reshape(shape)
        head = slice(g * HEAD_SIZE, (g + 1) * HEAD_SIZE)
        cached = lax.dot_general(
            q.reshape(flat).astype(BF16),
            s.kc[:, :, head],
            (((2,), (2,)), ((0,), (0,))),
            preferred_element_type=F32,
        )
        live = slots_lane < s.lengths[...]
        cached = jnp.where(live, cached * scale, MASKED)
        fresh0 = jnp.sum(q * k[:, 0:1], axis=-1, keepdims=True) * scale
        fresh1 = jnp.sum(q * k[:, 1:2], axis=-1, keepdims=True) * scale
        fresh1 = jnp.where(second, fresh1, MASKED)
        fresh0 = fresh0.reshape(requests, 2 * group, 1)
        fresh1 = fresh1.reshape(requests, 2 * group, 1)
        top = jnp.maximum(
            jnp.max(cached, axis=-1, keepdims=True), jnp.maximum(fresh0, fresh1)
        )
        cached = jnp.where(live, jnp.exp(cached - top), 0.0)
        fresh0 = jnp.exp(fresh0 - top)
        fresh1 = jnp.where(second.reshape(requests, 2 * group, 1), jnp.exp(fresh1 - top), 0.0)
        totals = jnp.sum(cached, axis=-1, keepdims=True) + (fresh0 + fresh1)
        mixture = lax.dot_general(
            (cached / totals).astype(BF16),
            s.vc[:, :, head],
            (((2,), (1,)), ((0,), (0,))),
            preferred_element_type=F32,
        ).reshape(shape)
        weight0 = (fresh0 / totals).astype(BF16).astype(F32).reshape(requests, 2, group, 1)
        weight1 = (fresh1 / totals).astype(BF16).astype(F32).reshape(requests, 2, group, 1)
        mixture = mixture + (weight0 * v[:, 0:1] + weight1 * v[:, 1:2])
        s.q3[...] = mixture.reshape(rows, group, HEAD_SIZE)
        for h in range(group):
            at = g * group_cols + h * HEAD_SIZE
            s.att[e, :, at : at + HEAD_SIZE] = s.q3[:, h, :].astype(BF16)
        each(n, lambda i: g_copy(i, g).start())

    for g in range(kv_heads):
        attend(g)

    loads["wo"].wait()
    piece = min(chunk, half_out)
    pieces = half_out // piece

    def place(block, index):
        return (
            pl.ds(pl.multiple_of(lax.div(index, 2) * half_rows, half_rows), half_rows),
            pl.ds(
                pl.multiple_of(block * out_cols + lax.rem(index, 2) * half_out, 128), half_out
            ),
        )

    def one_copy(i):
        return remote(s.one_send.at[i], s.one_recv.at[i], s.o_s.at[i], s.o_r.at[i], tp=near)

    def two_copy(i):
        return remote(
            s.two_send.at[i, 1 - b1], s.two_recv.at[i], s.t_s.at[i], s.t_r.at[i], tp=far
        )

    def three_copy(i):
        p = partner(i)
        return remote(
            s.three_send.at[i], s.out.at[place(e, t)], s.h_s.at[i], s.h_r.at[i], ep=p
        )

    def four_copy(i, k, index):
        ref = s.out.at[place(partner(i), index)]
        return remote(ref, ref, s.r_s.at[i, k], s.r_r.at[i, k], tp=far if k == 1 else near)

    def project(i, own=False):
        if not own:
            for g in range(kv_heads):
                g_copy(i, g).wait_recv()
        p = partner(i)
        values = s.att[p]
        for k, side in enumerate((1 - b0, b0)):
            for c in range(pieces):
                columns = pl.ds(pl.multiple_of(side * half_out + c * piece, 128), piece)
                value = dot(values, s.wo[:, columns])
                columns = slice(c * piece, (c + 1) * piece)
                if k == 0:
                    s.one_send[i, :, columns] = value.astype(BF16)
                else:
                    s.acc[i, :, columns] = value
            if k == 0:
                one_copy(i).start()

    def add_near(i, own=False):
        one_copy(i).wait_recv()
        value = s.acc[i] + s.one_recv[i].astype(F32)
        for k in range(2):
            block = value[k * half_rows : (k + 1) * half_rows]
            s.two_wide[i, k] = block
            s.two_send[i, k] = block.astype(BF16)
        two_copy(i).start()

    def add_far(i, own=False):
        two_copy(i).wait_recv()
        value = (s.two_wide[i, b1] + s.two_recv[i].astype(F32)).astype(BF16)
        if own:
            s.out[place(e, t)] = value
        else:
            s.three_send[i] = value
            three_copy(i).start()

    def pass_on(i, own=False):
        if not own:
            ref = s.out.at[place(partner(i), t)]
            remote(ref, ref, s.h_s.at[i], s.h_r.at[i], ep=partner(i)).wait_recv()
        four_copy(i, 1, t).start()
        four_copy(i, 0, t).start()

    def pass_far(i, own=False):
        four_copy(i, 1, far).wait_recv()
        four_copy(i, 2, far).start()

    stages = (project, add_near, add_far, pass_on, pass_far)
    if n <= UNROLL_PEERS:
        for step in range(n + len(stages) - 1):
            for k, stage in enumerate(stages):
                if 0 <= step - k < n:
                    stage(step - k, own=step == k)
    else:
        for stage in stages:
            stage(0, own=True)
            each(n, stage)

    def last(i):
        four_copy(i, 0, near).wait_recv()
        four_copy(i, 2, across).wait_recv()

    last(0)
    each(n, last)
    final = pltpu.make_async_copy(s.out, s.out_hbm, s.load_sem.at[0])
    final.start()

    def drain(i):
        a_copy(i).wait_send()
        m_copy(i).wait_send()
        b_copy(i).wait_send()
        for c in range(q_chunks + kv_chunks):
            p_copy(i, c).wait_send()
        for g in range(kv_heads):
            g_copy(i, g).wait_send()
        three_copy(i).wait_send()
        for k in range(3):
            f_copy(i, k, t).wait_send()

    each(n, drain)

    def drain_tp(i):
        one_copy(i).wait_send()
        two_copy(i).wait_send()
        for k in range(3):
            four_copy(i, k, t).wait_send()

    drain_tp(0)
    each(n, drain_tp)
    for j in range(1, TP):
        s_copy(j).wait_send()
    final.wait()


def local(
    tokens,
    query_weight,
    key_weight,
    value_weight,
    output_weight,
    adapter_down_maps,
    adapter_up_maps,
    rotated_cache_keys,
    cached_value_rows,
    adapter_index,
    cached_lengths,
):
    n = lax.axis_size("ep")
    requests, steps, width = tokens.shape
    rows = requests * steps
    feat, q_cols = query_weight.shape
    kv_cols = key_weight.shape[1]
    all_cols = q_cols + 2 * kv_cols
    out_cols = output_weight.shape[1]
    half_out = out_cols // 2
    adapters, part, rank = adapter_down_maps.shape
    capacity = max(2, (2 * requests + n - 1) // n)
    slot_rows = max(16, -(-capacity * steps // 16) * 16)
    slots = n * slot_rows
    group = QUERY_HEADS // KEY_HEADS
    kv_heads = kv_cols // HEAD_SIZE
    chunks = all_cols // 512
    vmem = pltpu.VMEM
    dma = pltpu.SemaphoreType.DMA
    scratch = dict(
        tok=vmem((rows, width), BF16),
        nrm=vmem((rows, width), BF16),
        wq=vmem(query_weight.shape, BF16),
        wkv=vmem((feat, 2 * kv_cols), BF16),
        wo=vmem(output_weight.shape, BF16),
        dn=vmem((adapters, rank, part), BF16),
        up=vmem(adapter_up_maps.shape, BF16),
        kc=vmem(rotated_cache_keys.shape, BF16),
        vc=vmem(cached_value_rows.shape, BF16),
        x=vmem((n, rows, feat), BF16),
        b_send=vmem((n, slot_rows, part), BF16),
        b_recv=vmem((n, slot_rows, part), BF16),
        id_send=vmem((8, 128), jnp.int32),
        ids=vmem((n, 8, 128), jnp.int32),
        sh_send=vmem((slots, 128), F32),
        sh_recv=vmem((TP, slots, 128), F32),
        p_wide=vmem((n * rows, all_cols), F32),
        p_send=vmem((n, rows, all_cols), BF16),
        p_recv=vmem((n, rows, all_cols), BF16),
        tot=vmem((rows, all_cols), F32),
        cos=vmem((rows, HEAD_SIZE), F32),
        sin=vmem((rows, HEAD_SIZE), F32),
        lengths=vmem((requests, 2 * group, HEAD_SIZE), jnp.int32),
        q3=vmem((rows, group, HEAD_SIZE), F32),
        k3=vmem((rows, group, HEAD_SIZE), F32),
        v3=vmem((rows, group, HEAD_SIZE), F32),
        att=vmem((n, rows, q_cols), BF16),
        acc=vmem((n, rows, half_out), F32),
        one_send=vmem((n, rows, half_out), BF16),
        one_recv=vmem((n, rows, half_out), BF16),
        two_wide=vmem((n, 2, rows // 2, half_out), F32),
        two_send=vmem((n, 2, rows // 2, half_out), BF16),
        two_recv=vmem((n, rows // 2, half_out), BF16),
        three_send=vmem((n, rows // 2, half_out), BF16),
        out=vmem((rows, width), BF16),
        load_sem=dma((9,)),
        a_s=dma((n,)),
        a_r=dma((n,)),
        m_s=dma((n,)),
        m_r=dma((n,)),
        b_s=dma((n,)),
        b_r=dma((n,)),
        f_s=dma((n, 3)),
        f_r=dma((n, 3)),
        s_s=dma((TP,)),
        s_r=dma((TP,)),
        p_s=dma((n, chunks)),
        p_r=dma((n, chunks)),
        g_s=dma((n, kv_heads)),
        g_r=dma((n, kv_heads)),
        o_s=dma((n,)),
        o_r=dma((n,)),
        t_s=dma((n,)),
        t_r=dma((n,)),
        h_s=dma((n,)),
        h_r=dma((n,)),
        r_s=dma((n, 3)),
        r_r=dma((n, 3)),
    )
    operands = [
        "idx_ref",
        "len_ref",
        "tok_hbm",
        "wq_hbm",
        "wk_hbm",
        "wv_hbm",
        "wo_hbm",
        "dn_hbm",
        "up_hbm",
        "kc_hbm",
        "vc_hbm",
        "out_hbm",
    ]
    out = pl.pallas_call(
        functools.partial(body, n, operands + list(scratch)),
        out_shape=jax.ShapeDtypeStruct((rows, width), BF16),
        in_specs=[pl.BlockSpec(memory_space=pltpu.SMEM)] * 2
        + [pl.BlockSpec(memory_space=pl.ANY)] * 9,
        out_specs=pl.BlockSpec(memory_space=pl.ANY),
        scratch_shapes=list(scratch.values()),
        compiler_params=pltpu.CompilerParams(
            collective_id=0, has_side_effects=True, vmem_limit_bytes=60 * 2**20
        ),
        name="sublayer",
    )(
        adapter_index,
        cached_lengths,
        tokens.reshape(rows, width),
        query_weight,
        key_weight,
        value_weight,
        output_weight,
        jnp.swapaxes(adapter_down_maps, 1, 2),
        adapter_up_maps,
        rotated_cache_keys,
        cached_value_rows,
    )
    return out.reshape(tokens.shape)


def solution(mesh):
    return jax.shard_map(
        local,
        mesh=mesh,
        in_specs=(
            P(("groups", "ep"), None, None),
            P("ep", "tp"),
            P("ep", "tp"),
            P("ep", "tp"),
            P("tp", "ep"),
            P("ep", "tp", None),
            P("ep", None, "tp"),
            P(("groups", "ep"), None, "tp"),
            P(("groups", "ep"), None, "tp"),
            P(("groups", "ep")),
            P(("groups", "ep")),
        ),
        out_specs=P(("groups", "ep"), None, None),
        check_vma=False,
    )
```

```python
import functools
import math
import types

import jax
import jax.numpy as jnp
from jax import lax
from jax.experimental import pallas as pl
from jax.experimental.pallas import tpu as pltpu
from jax.sharding import PartitionSpec as P

QUERY_HEADS = 64
KEY_HEADS = 8
HEAD_SIZE = 128
EPSILON = 1e-05
THETA = 500000.0
MASKED = -1e30
MESH = pl.DeviceIdType.MESH
F32 = jnp.float32
BF16 = jnp.bfloat16
TP = 4
UNROLL_PEERS = 8


def each(count, body):
    if count <= UNROLL_PEERS:
        for i in range(1, count):
            body(i)
    else:

        @pl.loop(1, count)
        def _(i):
            body(i)


def dot(a, b):
    return jnp.dot(a, b, preferred_element_type=F32)


def body(n, names, *refs):
    s = types.SimpleNamespace(**dict(zip(names, refs)))
    e = lax.axis_index("ep")
    t = lax.axis_index("tp")
    rows, width = s.tok.shape
    requests = rows // 2
    half_rows = rows // 2
    feat = width // n
    half_feat = feat // 2
    slot_rows = s.b_recv.shape[1]
    part = s.b_recv.shape[2]
    q_cols = s.wq.shape[1]
    kv_cols = s.wkv.shape[1] // 2
    out_cols = s.wo.shape[1]
    half_out = out_cols // 2
    adapters = s.dn.shape[0]
    rank = s.dn.shape[1]
    kv_heads = kv_cols // HEAD_SIZE
    group = QUERY_HEADS // KEY_HEADS
    chunk = 512
    group_cols = group * HEAD_SIZE

    def partner(i):
        both = 0
        bit = 1
        while bit < n:
            both = both + bit * (lax.rem(lax.div(e, bit), 2) * ((i // bit) % 2))
            bit *= 2
        return e + i - 2 * both

    def tp_up(j):
        return lax.rem(t + j, TP)

    def tp_down(j):
        return lax.rem(t + TP - j, TP)

    def remote(src, dst, send, recv, ep=None, tp=None):
        return pltpu.make_async_remote_copy(
            src_ref=src,
            dst_ref=dst,
            send_sem=send,
            recv_sem=recv,
            device_id={"ep": e if ep is None else ep, "tp": t if tp is None else tp},
            device_id_type=MESH,
        )

    loads = {}
    for k, (name, src, dst) in enumerate(
        [
            ("tok", s.tok_hbm, s.tok),
            ("dn", s.dn_hbm, s.dn),
            ("wk", s.wk_hbm, s.wkv.at[:, :kv_cols]),
            ("wv", s.wv_hbm, s.wkv.at[:, kv_cols:]),
            ("wq", s.wq_hbm, s.wq),
            ("up", s.up_hbm, s.up),
            ("kc", s.kc_hbm, s.kc),
            ("vc", s.vc_hbm, s.vc),
            ("wo", s.wo_hbm, s.wo),
        ]
    ):
        loads[name] = pltpu.make_async_copy(src, dst, s.load_sem.at[k])
        loads[name].start()

    barrier = pltpu.get_barrier_semaphore()

    def greet(i):
        pl.semaphore_signal(
            barrier, inc=1, device_id={"ep": partner(i), "tp": t}, device_id_type=MESH
        )

    each(n, greet)
    for j in range(1, TP):
        pl.semaphore_signal(
            barrier, inc=1, device_id={"ep": e, "tp": tp_up(j)}, device_id_type=MESH
        )

    square = (1, rows, rows)
    sub = lax.broadcasted_iota(jnp.int32, square, 1)
    lane = lax.broadcasted_iota(jnp.int32, square, 2)
    sub_req = jnp.right_shift(sub, 1)
    lane_req = jnp.right_shift(lane, 1)
    slots = n * slot_rows

    def slots_of(flags):
        flags_sub = jnp.sum(jnp.where(sub == lane, flags, 0), axis=2, keepdims=True)
        before_lane = jnp.sum(jnp.where(sub_req < lane_req, flags_sub, 0), axis=1, keepdims=True)
        before_sub = jnp.sum(jnp.where(lane_req < sub_req, flags, 0), axis=2, keepdims=True)
        return (
            flags_sub,
            before_lane + (lane - 2 * lane_req)[:, :1],
            before_sub + (sub - 2 * sub_req)[:, :, :1],
        )

    tile_req = jnp.right_shift(lax.broadcasted_iota(jnp.int32, (8, 128), 1), 1)
    lane3 = lax.broadcasted_iota(jnp.int32, (rows, HEAD_SIZE), 0)
    position = jnp.zeros((rows, HEAD_SIZE), F32)
    own_ids = jnp.zeros((8, 128), jnp.int32)
    for r in range(requests):
        own_ids = jnp.where(tile_req == r, s.idx_ref[r], own_ids)
        length = s.len_ref[r]
        s.lengths[r] = jnp.full((2 * group, HEAD_SIZE), length, jnp.int32)
        position = jnp.where(jnp.right_shift(lane3, 1) == r, length.astype(F32), position)
    position = position + (lane3 - 2 * jnp.right_shift(lane3, 1)).astype(F32)
    s.id_send[...] = own_ids
    s.ids[e] = own_ids
    owners = lax.broadcasted_iota(jnp.int32, (n, 1, rows), 0)
    own_row = own_ids[:1, :rows].reshape(1, 1, rows) - owners * adapters
    flags = jnp.where((own_row >= 0) & (own_row < adapters), 1, 0)
    _, slot_lane, _ = slots_of(flags)
    placing = (lax.broadcasted_iota(jnp.int32, (n, slot_rows, rows), 1) == slot_lane) & (flags > 0)
    placing = jnp.where(placing, 1.0, 0.0).reshape(slots, rows)

    loads["tok"].wait()
    for r in range(0, rows, 16):
        wide = s.tok[r : r + 16, :].astype(F32)
        factor = lax.rsqrt(jnp.mean(wide * wide, axis=-1, keepdims=True) + EPSILON)
        s.nrm[r : r + 16, :] = (wide * factor).astype(BF16)

    pl.semaphore_wait(barrier, n - 1 + TP - 1)

    def quarter(block, index):
        return (
            block,
            pl.ds(pl.multiple_of(lax.rem(index, 2) * half_rows, half_rows), half_rows),
            pl.ds(pl.multiple_of(lax.div(index, 2) * half_feat, 128), half_feat),
        )

    def a_copy(i):
        p = partner(i)
        src = s.nrm.at[
            pl.ds(pl.multiple_of(lax.rem(t, 2) * half_rows, half_rows), half_rows),
            pl.ds(pl.multiple_of(p * feat + lax.div(t, 2) * half_feat, 128), half_feat),
        ]
        return remote(src, s.x.at[quarter(e, t)], s.a_s.at[i], s.a_r.at[i], ep=p)

    each(n, lambda i: a_copy(i).start())

    def m_copy(i):
        p = partner(i)
        return remote(s.id_send, s.ids.at[e], s.m_s.at[i], s.m_r.at[i], ep=p)

    each(n, lambda i: m_copy(i).start())

    own_part = s.nrm[:, pl.ds(pl.multiple_of(t * part, 128), part)]
    placed = dot(placing.astype(BF16), own_part).astype(BF16)
    s.b_send[...] = placed.reshape(n, slot_rows, part)

    def b_copy(i):
        p = partner(i)
        return remote(s.b_send.at[p], s.b_recv.at[e], s.b_s.at[i], s.b_r.at[i], ep=p)

    each(n, lambda i: b_copy(i).start())
    s.b_recv[e] = s.b_send[e]
    s.x[e] = s.nrm[:, pl.ds(pl.multiple_of(e * feat, 128), feat)]

    pair = lax.broadcasted_iota(jnp.int32, (rows, HEAD_SIZE), 1)
    upper = pair >= HEAD_SIZE // 2
    pair = jnp.where(upper, pair - HEAD_SIZE // 2, pair).astype(F32)
    angles = position * jnp.exp(pair * (-2.0 / HEAD_SIZE) * math.log(THETA))
    s.cos[...] = jnp.cos(angles)
    sine = jnp.sin(angles)
    s.sin[...] = jnp.where(upper, sine, -sine)

    b0 = lax.rem(t, 2)
    b1 = lax.div(t, 2)
    near = t + 1 - 2 * b0
    far = t + 2 - 4 * b1
    across = near + 2 - 4 * b1

    def f_copy(i, k, index):
        ref = s.x.at[quarter(partner(i), index)]
        return remote(ref, ref, s.f_s.at[i, k], s.f_r.at[i, k], tp=far if k == 1 else near)

    def forward(i):
        ref = s.x.at[quarter(partner(i), t)]
        remote(ref, ref, s.a_s.at[i], s.a_r.at[i], ep=partner(i)).wait_recv()
        f_copy(i, 1, t).start()
        f_copy(i, 0, t).start()

    def forward_far(i):
        f_copy(i, 1, far).wait_recv()
        f_copy(i, 2, far).start()

    each(n, forward)
    each(n, forward_far)

    def b_in(i):
        m_copy(i).wait_recv()
        remote(
            s.b_send.at[partner(i)],
            s.b_recv.at[partner(i)],
            s.b_s.at[i],
            s.b_r.at[i],
            ep=partner(i),
        ).wait_recv()

    each(n, b_in)
    loads["dn"].wait()
    arrived = s.b_recv[...].reshape(slots, part)
    ids = s.ids[:, :1, :rows] - e * adapters
    flags = jnp.where((ids >= 0) & (ids < adapters), 1, 0)
    flags_sub, slot_lane, slot_sub = slots_of(flags)
    taken = (lax.broadcasted_iota(jnp.int32, (n, slot_rows, rows), 1) == slot_lane) & (flags > 0)
    labels = jnp.sum(jnp.where(taken, ids, 0), axis=2, keepdims=True)
    labels = jnp.broadcast_to(labels, (n, slot_rows, 128)).reshape(slots, 128)
    lane_slot = lax.broadcasted_iota(jnp.int32, (slots, 128), 1)
    offset = jnp.where(lane_slot >= rank, 1, 0)
    down = lax.dot_general(
        arrived,
        s.dn[...].reshape(adapters * rank, part),
        (((1,), (1,)), ((), ())),
        preferred_element_type=F32,
    )
    total = jnp.zeros((slots, 128), F32)
    for a in range(adapters // 2):
        block = down[:, 128 * a : 128 * (a + 1)]
        total = total + jnp.where(labels == 2 * a + offset, block, 0.0)
    s.sh_send[...] = total + pltpu.roll(total, rank, 1)

    def s_copy(j):
        return remote(s.sh_send, s.sh_recv.at[j], s.s_s.at[j], s.s_r.at[j], tp=tp_up(j))

    for j in range(1, TP):
        s_copy(j).start()

    def f_in(i):
        f_copy(i, 0, near).wait_recv()
        f_copy(i, 2, across).wait_recv()

    each(n, f_in)
    loads["wk"].wait()
    loads["wv"].wait()
    row_block = s.x[...].reshape(n * rows, feat)

    paired = n == 4

    def p_copy(i, c):
        p = partner(i)
        columns = pl.ds(c * chunk, chunk)
        return remote(
            s.p_send.at[p, :, columns],
            s.p_recv.at[i, :, columns],
            s.p_s.at[i, c],
            s.p_r.at[i, c],
            ep=partner(1) if paired and i == 3 else p,
        )

    def ship(c, value):
        columns = slice(c * chunk, (c + 1) * chunk)
        s.p_wide[:, columns] = value
        s.p_send[:, :, columns] = value.astype(BF16).reshape(n, rows, chunk)
        if paired:
            p_copy(1, c).start()
            p_copy(3, c).start()
        else:
            each(n, lambda i: p_copy(i, c).start())

    def ship_far(c):
        columns = slice(c * chunk, (c + 1) * chunk)
        p_copy(3, c).wait_recv()
        p = partner(2)
        value = s.p_wide[pl.ds(pl.multiple_of(p * rows, rows), rows), columns]
        value = value + s.p_recv[3, :, columns].astype(F32)
        s.p_send[p, :, columns] = value.astype(BF16)
        p_copy(2, c).start()

    q_chunks = q_cols // chunk
    kv_chunks = 2 * kv_cols // chunk
    for c in range(kv_chunks):
        ship(q_chunks + c, dot(row_block, s.wkv[:, c * chunk : (c + 1) * chunk]))

    loads["wq"].wait()
    for c in range(q_chunks):
        columns = slice(c * chunk, (c + 1) * chunk)
        s.p_wide[:, columns] = dot(row_block, s.wq[:, columns])
    if paired:
        for c in range(kv_chunks):
            ship_far(q_chunks + c)

    for j in range(1, TP):
        s_copy(j).wait_recv()
        total_j = s.sh_recv[j]
        sh = s.sh_send[...] + total_j if j == 1 else sh + total_j
    sh = sh.astype(BF16)
    spread = jnp.concatenate(
        [
            jnp.where(labels == 2 * a + offset, sh, jnp.zeros_like(sh))
            for a in range(adapters // 2)
        ],
        axis=1,
    )
    loads["up"].wait()
    block = lax.broadcasted_iota(jnp.int32, (n, rows, 1), 0) * slot_rows
    codes = jnp.where(flags_sub > 0, slot_sub + block, -1)
    returning = lax.broadcasted_iota(jnp.int32, (n, rows, slots), 2) == codes
    returning = jnp.where(returning, 1.0, 0.0).reshape(n * rows, slots).astype(BF16)
    up = s.up[...].reshape(adapters * rank, q_cols)
    for c in range(q_chunks):
        columns = slice(c * chunk, (c + 1) * chunk)
        delta = dot(spread, up[:, columns]).astype(BF16)
        ship(c, s.p_wide[:, columns] + dot(returning, delta))
    if paired:
        for c in range(q_chunks):
            ship_far(c)

    def p_sum(c):
        columns = slice(c * chunk, (c + 1) * chunk)
        sources = range(1, 3 if paired else n)
        if paired:
            for i in sources:
                p_copy(i, c).wait_recv()
        else:
            each(n, lambda i: p_copy(i, c).wait_recv())
        value = s.p_wide[pl.ds(pl.multiple_of(e * rows, rows), rows), columns]
        for i in sources:
            value = value + s.p_recv[i, :, columns].astype(F32)
        s.tot[:, columns] = value

    def rotate(value):
        return (value * s.cos[...] + pltpu.roll(value, HEAD_SIZE // 2, 1) * s.sin[...]).astype(BF16)

    for c in range(kv_chunks):
        p_sum(q_chunks + c)
    loads["kc"].wait()
    loads["vc"].wait()
    scale = 1.0 / math.sqrt(HEAD_SIZE)
    shape = (requests, 2, group, HEAD_SIZE)
    flat = (requests, 2 * group, HEAD_SIZE)
    slots_lane = lax.broadcasted_iota(jnp.int32, flat, 2)
    second = lax.broadcasted_iota(jnp.int32, (requests, 2, group, 1), 1) == 1

    def g_copy(i, g):
        columns = pl.ds(g * group_cols, group_cols)
        if paired and i == 3:
            ref = s.att.at[partner(2), :, columns]
            return remote(ref, ref, s.g_s.at[i, g], s.g_r.at[i, g], ep=partner(1))
        ref = s.att.at[e, :, columns]
        return remote(ref, ref, s.g_s.at[i, g], s.g_r.at[i, g], ep=partner(i))

    def g_wait(i, g):
        g_copy(i, g).wait_recv()
        if paired and i == 2:
            g_copy(3, g).start()

    def attend(g):
        for c in range(g * group_cols // chunk, (g + 1) * group_cols // chunk):
            p_sum(c)
        base = q_cols + g * HEAD_SIZE
        key = rotate(s.tot[:, base : base + HEAD_SIZE]).astype(F32)
        value = s.tot[:, base + kv_cols : base + kv_cols + HEAD_SIZE].astype(BF16).astype(F32)
        for h in range(group):
            at = g * group_cols + h * HEAD_SIZE
            s.q3[:, h, :] = rotate(s.tot[:, at : at + HEAD_SIZE]).astype(F32)
            s.k3[:, h, :] = key
            s.v3[:, h, :] = value
        q = s.q3[...].reshape(shape)
        k = s.k3[...].reshape(shape)
        v = s.v3[...].reshape(shape)
        head = slice(g * HEAD_SIZE, (g + 1) * HEAD_SIZE)
        cached = lax.dot_general(
            q.reshape(flat).astype(BF16),
            s.kc[:, :, head],
            (((2,), (2,)), ((0,), (0,))),
            preferred_element_type=F32,
        )
        live = slots_lane < s.lengths[...]
        cached = jnp.where(live, cached * scale, MASKED)
        fresh0 = jnp.sum(q * k[:, 0:1], axis=-1, keepdims=True) * scale
        fresh1 = jnp.sum(q * k[:, 1:2], axis=-1, keepdims=True) * scale
        fresh1 = jnp.where(second, fresh1, MASKED)
        fresh0 = fresh0.reshape(requests, 2 * group, 1)
        fresh1 = fresh1.reshape(requests, 2 * group, 1)
        top = jnp.maximum(
            jnp.max(cached, axis=-1, keepdims=True), jnp.maximum(fresh0, fresh1)
        )
        cached = jnp.where(live, jnp.exp(cached - top), 0.0)
        fresh0 = jnp.exp(fresh0 - top)
        fresh1 = jnp.where(second.reshape(requests, 2 * group, 1), jnp.exp(fresh1 - top), 0.0)
        totals = jnp.sum(cached, axis=-1, keepdims=True) + (fresh0 + fresh1)
        mixture = lax.dot_general(
            (cached / totals).astype(BF16),
            s.vc[:, :, head],
            (((2,), (1,)), ((0,), (0,))),
            preferred_element_type=F32,
        ).reshape(shape)
        weight0 = (fresh0 / totals).astype(BF16).astype(F32).reshape(requests, 2, group, 1)
        weight1 = (fresh1 / totals).astype(BF16).astype(F32).reshape(requests, 2, group, 1)
        mixture = mixture + (weight0 * v[:, 0:1] + weight1 * v[:, 1:2])
        s.q3[...] = mixture.reshape(rows, group, HEAD_SIZE)
        for h in range(group):
            at = g * group_cols + h * HEAD_SIZE
            s.att[e, :, at : at + HEAD_SIZE] = s.q3[:, h, :].astype(BF16)
        if paired:
            g_copy(2, g).start()
            g_copy(1, g).start()
        else:
            each(n, lambda i: g_copy(i, g).start())

    piece = min(chunk, out_cols)
    pieces = out_cols // piece

    def place(block, index):
        return (
            pl.ds(pl.multiple_of(lax.div(index, 2) * half_rows, half_rows), half_rows),
            pl.ds(
                pl.multiple_of(block * out_cols + lax.rem(index, 2) * half_out, 128), half_out
            ),
        )

    def one_copy(i, j):
        p = tp_up(j)
        return remote(
            s.one_send.at[i, p], s.one_recv.at[i, j], s.o_s.at[i, j], s.o_r.at[i, j], tp=p
        )

    def three_copy(i):
        p = partner(i)
        return remote(
            s.three_send.at[i], s.out.at[place(e, t)], s.h_s.at[i], s.h_r.at[i], ep=p
        )

    def four_copy(i, j, index):
        ref = s.out.at[place(partner(i), index)]
        return remote(ref, ref, s.r_s.at[i, j], s.r_r.at[i, j], tp=tp_up(j))

    def project_head(i, g):
        values = s.att[partner(i), :, g * group_cols : (g + 1) * group_cols]
        for c in range(pieces):
            columns = slice(c * piece, (c + 1) * piece)
            value = dot(values, s.wo[g * group_cols : (g + 1) * group_cols, columns])
            if g > 0:
                value = s.acc[i, :, columns] + value
            s.acc[i, :, columns] = value

    def project_first(i):
        for g in range(kv_heads - 1):
            g_wait(i, g)
            project_head(i, g)

    def project(i, own=False):
        if not own:
            g_wait(i, kv_heads - 1)
        project_head(i, kv_heads - 1)
        for index in range(TP):
            k, side = index // 2, index % 2
            s.one_send[i, index] = s.acc[
                i,
                k * half_rows : (k + 1) * half_rows,
                side * half_out : (side + 1) * half_out,
            ].astype(BF16)
        for j in range(1, TP):
            one_copy(i, j).start()

    def add_up(i, own=False):
        value = s.acc[
            i,
            pl.ds(pl.multiple_of(b1 * half_rows, half_rows), half_rows),
            pl.ds(pl.multiple_of(b0 * half_out, 128), half_out),
        ]
        for j in range(1, TP):
            one_copy(i, j).wait_recv()
            value = value + s.one_recv[i, j].astype(F32)
        value = value.astype(BF16)
        if own:
            s.out[place(e, t)] = value
        else:
            s.three_send[i] = value
            three_copy(i).start()

    def pass_on(i, own=False):
        if not own:
            ref = s.out.at[place(partner(i), t)]
            remote(ref, ref, s.h_s.at[i], s.h_r.at[i], ep=partner(i)).wait_recv()
        for j in range(1, TP):
            four_copy(i, j, t).start()

    for g in range(kv_heads):
        attend(g)
        if g == 0:
            loads["wo"].wait()
        if g < kv_heads - 1:
            project_head(0, g)
    each(n, project_first)

    stages = (project, add_up, pass_on)
    if n <= UNROLL_PEERS:
        for step in range(n + len(stages) - 1):
            for k, stage in enumerate(stages):
                if 0 <= step - k < n:
                    stage(step - k, own=step == k)
    else:
        for stage in stages:
            stage(0, own=True)
            each(n, stage)

    def last(i):
        for j in range(1, TP):
            four_copy(i, j, tp_down(j)).wait_recv()

    last(0)
    each(n, last)
    final = pltpu.make_async_copy(s.out, s.out_hbm, s.load_sem.at[0])
    final.start()

    def drain(i):
        a_copy(i).wait_send()
        m_copy(i).wait_send()
        b_copy(i).wait_send()
        for c in range(q_chunks + kv_chunks):
            p_copy(i, c).wait_send()
        for g in range(kv_heads):
            g_copy(i, g).wait_send()
        three_copy(i).wait_send()
        for k in range(3):
            f_copy(i, k, t).wait_send()

    each(n, drain)

    def drain_tp(i):
        for j in range(1, TP):
            one_copy(i, j).wait_send()
            four_copy(i, j, t).wait_send()

    drain_tp(0)
    each(n, drain_tp)
    for j in range(1, TP):
        s_copy(j).wait_send()
    final.wait()


def local(
    tokens,
    query_weight,
    key_weight,
    value_weight,
    output_weight,
    adapter_down_maps,
    adapter_up_maps,
    rotated_cache_keys,
    cached_value_rows,
    adapter_index,
    cached_lengths,
):
    n = lax.axis_size("ep")
    requests, steps, width = tokens.shape
    rows = requests * steps
    feat, q_cols = query_weight.shape
    kv_cols = key_weight.shape[1]
    all_cols = q_cols + 2 * kv_cols
    out_cols = output_weight.shape[1]
    half_out = out_cols // 2
    adapters, part, rank = adapter_down_maps.shape
    capacity = max(2, (2 * requests + n - 1) // n)
    slot_rows = max(16, -(-capacity * steps // 16) * 16)
    slots = n * slot_rows
    group = QUERY_HEADS // KEY_HEADS
    kv_heads = kv_cols // HEAD_SIZE
    chunks = all_cols // 512
    vmem = pltpu.VMEM
    dma = pltpu.SemaphoreType.DMA
    scratch = dict(
        tok=vmem((rows, width), BF16),
        nrm=vmem((rows, width), BF16),
        wq=vmem(query_weight.shape, BF16),
        wkv=vmem((feat, 2 * kv_cols), BF16),
        wo=vmem(output_weight.shape, BF16),
        dn=vmem((adapters, rank, part), BF16),
        up=vmem(adapter_up_maps.shape, BF16),
        kc=vmem(rotated_cache_keys.shape, BF16),
        vc=vmem(cached_value_rows.shape, BF16),
        x=vmem((n, rows, feat), BF16),
        b_send=vmem((n, slot_rows, part), BF16),
        b_recv=vmem((n, slot_rows, part), BF16),
        id_send=vmem((8, 128), jnp.int32),
        ids=vmem((n, 8, 128), jnp.int32),
        sh_send=vmem((slots, 128), F32),
        sh_recv=vmem((TP, slots, 128), F32),
        p_wide=vmem((n * rows, all_cols), F32),
        p_send=vmem((n, rows, all_cols), BF16),
        p_recv=vmem((n, rows, all_cols), BF16),
        tot=vmem((rows, all_cols), F32),
        cos=vmem((rows, HEAD_SIZE), F32),
        sin=vmem((rows, HEAD_SIZE), F32),
        lengths=vmem((requests, 2 * group, HEAD_SIZE), jnp.int32),
        q3=vmem((rows, group, HEAD_SIZE), F32),
        k3=vmem((rows, group, HEAD_SIZE), F32),
        v3=vmem((rows, group, HEAD_SIZE), F32),
        att=vmem((n, rows, q_cols), BF16),
        acc=vmem((n, rows, out_cols), F32),
        one_send=vmem((n, TP, rows // 2, half_out), BF16),
        one_recv=vmem((n, TP, rows // 2, half_out), BF16),
        three_send=vmem((n, rows // 2, half_out), BF16),
        out=vmem((rows, width), BF16),
        load_sem=dma((9,)),
        a_s=dma((n,)),
        a_r=dma((n,)),
        m_s=dma((n,)),
        m_r=dma((n,)),
        b_s=dma((n,)),
        b_r=dma((n,)),
        f_s=dma((n, 3)),
        f_r=dma((n, 3)),
        s_s=dma((TP,)),
        s_r=dma((TP,)),
        p_s=dma((n, chunks)),
        p_r=dma((n, chunks)),
        g_s=dma((n, kv_heads)),
        g_r=dma((n, kv_heads)),
        o_s=dma((n, TP)),
        o_r=dma((n, TP)),
        h_s=dma((n,)),
        h_r=dma((n,)),
        r_s=dma((n, TP)),
        r_r=dma((n, TP)),
    )
    operands = [
        "idx_ref",
        "len_ref",
        "tok_hbm",
        "wq_hbm",
        "wk_hbm",
        "wv_hbm",
        "wo_hbm",
        "dn_hbm",
        "up_hbm",
        "kc_hbm",
        "vc_hbm",
        "out_hbm",
    ]
    out = pl.pallas_call(
        functools.partial(body, n, operands + list(scratch)),
        out_shape=jax.ShapeDtypeStruct((rows, width), BF16),
        in_specs=[pl.BlockSpec(memory_space=pltpu.SMEM)] * 2
        + [pl.BlockSpec(memory_space=pl.ANY)] * 9,
        out_specs=pl.BlockSpec(memory_space=pl.ANY),
        scratch_shapes=list(scratch.values()),
        compiler_params=pltpu.CompilerParams(
            collective_id=0, has_side_effects=True, vmem_limit_bytes=60 * 2**20
        ),
        name="sublayer",
    )(
        adapter_index,
        cached_lengths,
        tokens.reshape(rows, width),
        query_weight,
        key_weight,
        value_weight,
        output_weight,
        jnp.swapaxes(adapter_down_maps, 1, 2),
        adapter_up_maps,
        rotated_cache_keys,
        cached_value_rows,
    )
    return out.reshape(tokens.shape)


def solution(mesh):
    return jax.shard_map(
        local,
        mesh=mesh,
        in_specs=(
            P(("groups", "ep"), None, None),
            P("ep", "tp"),
            P("ep", "tp"),
            P("ep", "tp"),
            P("tp", "ep"),
            P("ep", "tp", None),
            P("ep", None, "tp"),
            P(("groups", "ep"), None, "tp"),
            P(("groups", "ep"), None, "tp"),
            P(("groups", "ep")),
            P(("groups", "ep")),
        ),
        out_specs=P(("groups", "ep"), None, None),
        check_vma=False,
    )
```

```python
import functools
import math
import types

import jax
import jax.numpy as jnp
from jax import lax
from jax.experimental import pallas as pl
from jax.experimental.pallas import tpu as pltpu
from jax.sharding import PartitionSpec as P

QUERY_HEADS = 64
KEY_HEADS = 8
HEAD_SIZE = 128
EPSILON = 1e-05
THETA = 500000.0
MASKED = -1e30
MESH = pl.DeviceIdType.MESH
F32 = jnp.float32
BF16 = jnp.bfloat16
TP = 4
UNROLL_PEERS = 8


def each(count, body):
    if count <= UNROLL_PEERS:
        for i in range(1, count):
            body(i)
    else:

        @pl.loop(1, count)
        def _(i):
            body(i)


def dot(a, b):
    return jnp.dot(a, b, preferred_element_type=F32)


def body(n, names, *refs):
    s = types.SimpleNamespace(**dict(zip(names, refs)))
    e = lax.axis_index("ep")
    t = lax.axis_index("tp")
    rows, width = s.tok.shape
    requests = rows // 2
    half_rows = rows // 2
    feat = width // n
    half_feat = feat // 2
    slot_rows = s.b_recv.shape[1]
    part = s.b_recv.shape[2]
    q_cols = s.wq.shape[1]
    kv_cols = s.wkv.shape[1] // 2
    out_cols = s.wo.shape[1]
    half_out = out_cols // 2
    adapters = s.dn.shape[0]
    rank = s.dn.shape[1]
    kv_heads = kv_cols // HEAD_SIZE
    group = QUERY_HEADS // KEY_HEADS
    chunk = 512
    group_cols = group * HEAD_SIZE

    def partner(i):
        both = 0
        bit = 1
        while bit < n:
            both = both + bit * (lax.rem(lax.div(e, bit), 2) * ((i // bit) % 2))
            bit *= 2
        return e + i - 2 * both

    def tp_up(j):
        return lax.rem(t + j, TP)

    def tp_down(j):
        return lax.rem(t + TP - j, TP)

    def remote(src, dst, send, recv, ep=None, tp=None):
        return pltpu.make_async_remote_copy(
            src_ref=src,
            dst_ref=dst,
            send_sem=send,
            recv_sem=recv,
            device_id={"ep": e if ep is None else ep, "tp": t if tp is None else tp},
            device_id_type=MESH,
        )

    loads = {}
    for k, (name, src, dst) in enumerate(
        [
            ("tok", s.tok_hbm, s.tok),
            ("dn", s.dn_hbm, s.dn),
            ("wk", s.wk_hbm, s.wkv.at[:, :kv_cols]),
            ("wv", s.wv_hbm, s.wkv.at[:, kv_cols:]),
            ("wq", s.wq_hbm, s.wq),
            ("up", s.up_hbm, s.up),
            ("kc", s.kc_hbm, s.kc),
            ("vc", s.vc_hbm, s.vc),
            ("wo", s.wo_hbm, s.wo),
        ]
    ):
        loads[name] = pltpu.make_async_copy(src, dst, s.load_sem.at[k])
        loads[name].start()

    barrier = pltpu.get_barrier_semaphore()

    def greet(i):
        pl.semaphore_signal(
            barrier, inc=1, device_id={"ep": partner(i), "tp": t}, device_id_type=MESH
        )

    each(n, greet)
    for j in range(1, TP):
        pl.semaphore_signal(
            barrier, inc=1, device_id={"ep": e, "tp": tp_up(j)}, device_id_type=MESH
        )

    square = (1, rows, rows)
    sub = lax.broadcasted_iota(jnp.int32, square, 1)
    lane = lax.broadcasted_iota(jnp.int32, square, 2)
    sub_req = jnp.right_shift(sub, 1)
    lane_req = jnp.right_shift(lane, 1)
    slots = n * slot_rows

    def slots_of(flags):
        flags_sub = jnp.sum(jnp.where(sub == lane, flags, 0), axis=2, keepdims=True)
        before_lane = jnp.sum(jnp.where(sub_req < lane_req, flags_sub, 0), axis=1, keepdims=True)
        before_sub = jnp.sum(jnp.where(lane_req < sub_req, flags, 0), axis=2, keepdims=True)
        return (
            flags_sub,
            before_lane + (lane - 2 * lane_req)[:, :1],
            before_sub + (sub - 2 * sub_req)[:, :, :1],
        )

    tile_req = jnp.right_shift(lax.broadcasted_iota(jnp.int32, (8, 128), 1), 1)
    lane3 = lax.broadcasted_iota(jnp.int32, (rows, HEAD_SIZE), 0)
    position = jnp.zeros((rows, HEAD_SIZE), F32)
    own_ids = jnp.zeros((8, 128), jnp.int32)
    for r in range(requests):
        own_ids = jnp.where(tile_req == r, s.idx_ref[r], own_ids)
        length = s.len_ref[r]
        s.lengths[r] = jnp.full((2 * group, HEAD_SIZE), length, jnp.int32)
        position = jnp.where(jnp.right_shift(lane3, 1) == r, length.astype(F32), position)
    position = position + (lane3 - 2 * jnp.right_shift(lane3, 1)).astype(F32)
    s.id_send[...] = own_ids
    s.ids[e] = own_ids
    owners = lax.broadcasted_iota(jnp.int32, (n, 1, rows), 0)
    own_row = own_ids[:1, :rows].reshape(1, 1, rows) - owners * adapters
    flags = jnp.where((own_row >= 0) & (own_row < adapters), 1, 0)
    _, slot_lane, _ = slots_of(flags)
    placing = (lax.broadcasted_iota(jnp.int32, (n, slot_rows, rows), 1) == slot_lane) & (flags > 0)
    placing = jnp.where(placing, 1.0, 0.0).reshape(slots, rows)

    loads["tok"].wait()
    for r in range(0, rows, 16):
        wide = s.tok[r : r + 16, :].astype(F32)
        factor = lax.rsqrt(jnp.mean(wide * wide, axis=-1, keepdims=True) + EPSILON)
        s.nrm[r : r + 16, :] = (wide * factor).astype(BF16)

    pl.semaphore_wait(barrier, n - 1 + TP - 1)

    def quarter(block, index):
        return (
            block,
            pl.ds(pl.multiple_of(lax.rem(index, 2) * half_rows, half_rows), half_rows),
            pl.ds(pl.multiple_of(lax.div(index, 2) * half_feat, 128), half_feat),
        )

    def a_copy(i):
        p = partner(i)
        src = s.nrm.at[
            pl.ds(pl.multiple_of(lax.rem(t, 2) * half_rows, half_rows), half_rows),
            pl.ds(pl.multiple_of(p * feat + lax.div(t, 2) * half_feat, 128), half_feat),
        ]
        return remote(src, s.x.at[quarter(e, t)], s.a_s.at[i], s.a_r.at[i], ep=p)

    each(n, lambda i: a_copy(i).start())

    def m_copy(i):
        p = partner(i)
        return remote(s.id_send, s.ids.at[e], s.m_s.at[i], s.m_r.at[i], ep=p)

    each(n, lambda i: m_copy(i).start())

    own_part = s.nrm[:, pl.ds(pl.multiple_of(t * part, 128), part)]
    placed = dot(placing.astype(BF16), own_part).astype(BF16)
    s.b_send[...] = placed.reshape(n, slot_rows, part)

    def b_copy(i):
        p = partner(i)
        return remote(s.b_send.at[p], s.b_recv.at[e], s.b_s.at[i], s.b_r.at[i], ep=p)

    each(n, lambda i: b_copy(i).start())
    s.b_recv[e] = s.b_send[e]
    s.x[e] = s.nrm[:, pl.ds(pl.multiple_of(e * feat, 128), feat)]

    pair = lax.broadcasted_iota(jnp.int32, (rows, HEAD_SIZE), 1)
    upper = pair >= HEAD_SIZE // 2
    pair = jnp.where(upper, pair - HEAD_SIZE // 2, pair).astype(F32)
    angles = position * jnp.exp(pair * (-2.0 / HEAD_SIZE) * math.log(THETA))
    s.cos[...] = jnp.cos(angles)
    sine = jnp.sin(angles)
    s.sin[...] = jnp.where(upper, sine, -sine)

    b0 = lax.rem(t, 2)
    b1 = lax.div(t, 2)
    near = t + 1 - 2 * b0
    far = t + 2 - 4 * b1
    across = near + 2 - 4 * b1

    def f_copy(i, k, index):
        ref = s.x.at[quarter(partner(i), index)]
        return remote(ref, ref, s.f_s.at[i, k], s.f_r.at[i, k], tp=far if k == 1 else near)

    def forward(i):
        ref = s.x.at[quarter(partner(i), t)]
        remote(ref, ref, s.a_s.at[i], s.a_r.at[i], ep=partner(i)).wait_recv()
        f_copy(i, 1, t).start()
        f_copy(i, 0, t).start()

    def forward_far(i):
        f_copy(i, 1, far).wait_recv()
        f_copy(i, 2, far).start()

    each(n, forward)
    each(n, forward_far)

    def f_in(i):
        f_copy(i, 0, near).wait_recv()
        f_copy(i, 2, across).wait_recv()

    each(n, f_in)
    loads["wk"].wait()
    loads["wv"].wait()
    row_block = s.x[...].reshape(n * rows, feat)

    paired = n == 4

    def p_copy(i, c):
        p = partner(i)
        columns = pl.ds(c * chunk, chunk)
        return remote(
            s.p_send.at[p, :, columns],
            s.p_recv.at[i, :, columns],
            s.p_s.at[i, c],
            s.p_r.at[i, c],
            ep=partner(1) if paired and i == 3 else p,
        )

    def ship(c, value):
        columns = slice(c * chunk, (c + 1) * chunk)
        s.p_wide[:, columns] = value
        s.p_send[:, :, columns] = value.astype(BF16).reshape(n, rows, chunk)
        if paired:
            p_copy(1, c).start()
            p_copy(3, c).start()
        else:
            each(n, lambda i: p_copy(i, c).start())

    def ship_far(c):
        columns = slice(c * chunk, (c + 1) * chunk)
        p_copy(3, c).wait_recv()
        p = partner(2)
        value = s.p_wide[pl.ds(pl.multiple_of(p * rows, rows), rows), columns]
        value = value + s.p_recv[3, :, columns].astype(F32)
        s.p_send[p, :, columns] = value.astype(BF16)
        p_copy(2, c).start()

    q_chunks = q_cols // chunk
    kv_chunks = 2 * kv_cols // chunk
    for c in range(kv_chunks):
        ship(q_chunks + c, dot(row_block, s.wkv[:, c * chunk : (c + 1) * chunk]))

    loads["wq"].wait()
    for c in range(q_chunks):
        columns = slice(c * chunk, (c + 1) * chunk)
        s.p_wide[:, columns] = dot(row_block, s.wq[:, columns])

    def b_in(i):
        m_copy(i).wait_recv()
        remote(
            s.b_send.at[partner(i)],
            s.b_recv.at[partner(i)],
            s.b_s.at[i],
            s.b_r.at[i],
            ep=partner(i),
        ).wait_recv()

    each(n, b_in)
    loads["dn"].wait()
    arrived = s.b_recv[...].reshape(slots, part)
    ids = s.ids[:, :1, :rows] - e * adapters
    flags = jnp.where((ids >= 0) & (ids < adapters), 1, 0)
    flags_sub, slot_lane, slot_sub = slots_of(flags)
    taken = (lax.broadcasted_iota(jnp.int32, (n, slot_rows, rows), 1) == slot_lane) & (flags > 0)
    labels = jnp.sum(jnp.where(taken, ids, 0), axis=2, keepdims=True)
    labels = jnp.broadcast_to(labels, (n, slot_rows, 128)).reshape(slots, 128)
    lane_slot = lax.broadcasted_iota(jnp.int32, (slots, 128), 1)
    offset = jnp.where(lane_slot >= rank, 1, 0)
    down = lax.dot_general(
        arrived,
        s.dn[...].reshape(adapters * rank, part),
        (((1,), (1,)), ((), ())),
        preferred_element_type=F32,
    )
    total = jnp.zeros((slots, 128), F32)
    for a in range(adapters // 2):
        block = down[:, 128 * a : 128 * (a + 1)]
        total = total + jnp.where(labels == 2 * a + offset, block, 0.0)
    s.sh_send[...] = total + pltpu.roll(total, rank, 1)

    def s_copy(j):
        return remote(s.sh_send, s.sh_recv.at[j], s.s_s.at[j], s.s_r.at[j], tp=tp_up(j))

    for j in range(1, TP):
        s_copy(j).start()

    if paired:
        for c in range(kv_chunks):
            ship_far(q_chunks + c)

    for j in range(1, TP):
        s_copy(j).wait_recv()
        total_j = s.sh_recv[j]
        sh = s.sh_send[...] + total_j if j == 1 else sh + total_j
    sh = sh.astype(BF16)
    spread = jnp.concatenate(
        [
            jnp.where(labels == 2 * a + offset, sh, jnp.zeros_like(sh))
            for a in range(adapters // 2)
        ],
        axis=1,
    )
    loads["up"].wait()
    block = lax.broadcasted_iota(jnp.int32, (n, rows, 1), 0) * slot_rows
    codes = jnp.where(flags_sub > 0, slot_sub + block, -1)
    returning = lax.broadcasted_iota(jnp.int32, (n, rows, slots), 2) == codes
    returning = jnp.where(returning, 1.0, 0.0).reshape(n * rows, slots).astype(BF16)
    up = s.up[...].reshape(adapters * rank, q_cols)
    for c in range(q_chunks):
        columns = slice(c * chunk, (c + 1) * chunk)
        delta = dot(spread, up[:, columns]).astype(BF16)
        ship(c, s.p_wide[:, columns] + dot(returning, delta))
    if paired:
        for c in range(q_chunks):
            ship_far(c)

    def p_sum(c):
        columns = slice(c * chunk, (c + 1) * chunk)
        sources = range(1, 3 if paired else n)
        if paired:
            for i in sources:
                p_copy(i, c).wait_recv()
        else:
            each(n, lambda i: p_copy(i, c).wait_recv())
        value = s.p_wide[pl.ds(pl.multiple_of(e * rows, rows), rows), columns]
        for i in sources:
            value = value + s.p_recv[i, :, columns].astype(F32)
        s.tot[:, columns] = value

    def rotate(value):
        return (value * s.cos[...] + pltpu.roll(value, HEAD_SIZE // 2, 1) * s.sin[...]).astype(BF16)

    for c in range(kv_chunks):
        p_sum(q_chunks + c)
    loads["kc"].wait()
    loads["vc"].wait()
    scale = 1.0 / math.sqrt(HEAD_SIZE)
    shape = (requests, 2, group, HEAD_SIZE)
    flat = (requests, 2 * group, HEAD_SIZE)
    slots_lane = lax.broadcasted_iota(jnp.int32, flat, 2)
    second = lax.broadcasted_iota(jnp.int32, (requests, 2, group, 1), 1) == 1

    def g_copy(i, g):
        columns = pl.ds(g * group_cols, group_cols)
        if paired and i == 3:
            ref = s.att.at[partner(2), :, columns]
            return remote(ref, ref, s.g_s.at[i, g], s.g_r.at[i, g], ep=partner(1))
        ref = s.att.at[e, :, columns]
        return remote(ref, ref, s.g_s.at[i, g], s.g_r.at[i, g], ep=partner(i))

    def g_wait(i, g):
        g_copy(i, g).wait_recv()
        if paired and i == 2:
            g_copy(3, g).start()

    def attend(g):
        for c in range(g * group_cols // chunk, (g + 1) * group_cols // chunk):
            p_sum(c)
        base = q_cols + g * HEAD_SIZE
        key = rotate(s.tot[:, base : base + HEAD_SIZE]).astype(F32)
        value = s.tot[:, base + kv_cols : base + kv_cols + HEAD_SIZE].astype(BF16).astype(F32)
        for h in range(group):
            at = g * group_cols + h * HEAD_SIZE
            s.q3[:, h, :] = rotate(s.tot[:, at : at + HEAD_SIZE]).astype(F32)
            s.k3[:, h, :] = key
            s.v3[:, h, :] = value
        q = s.q3[...].reshape(shape)
        k = s.k3[...].reshape(shape)
        v = s.v3[...].reshape(shape)
        head = slice(g * HEAD_SIZE, (g + 1) * HEAD_SIZE)
        cached = lax.dot_general(
            q.reshape(flat).astype(BF16),
            s.kc[:, :, head],
            (((2,), (2,)), ((0,), (0,))),
            preferred_element_type=F32,
        )
        live = slots_lane < s.lengths[...]
        cached = jnp.where(live, cached * scale, MASKED)
        fresh0 = jnp.sum(q * k[:, 0:1], axis=-1, keepdims=True) * scale
        fresh1 = jnp.sum(q * k[:, 1:2], axis=-1, keepdims=True) * scale
        fresh1 = jnp.where(second, fresh1, MASKED)
        fresh0 = fresh0.reshape(requests, 2 * group, 1)
        fresh1 = fresh1.reshape(requests, 2 * group, 1)
        top = jnp.maximum(
            jnp.max(cached, axis=-1, keepdims=True), jnp.maximum(fresh0, fresh1)
        )
        cached = jnp.where(live, jnp.exp(cached - top), 0.0)
        fresh0 = jnp.exp(fresh0 - top)
        fresh1 = jnp.where(second.reshape(requests, 2 * group, 1), jnp.exp(fresh1 - top), 0.0)
        totals = jnp.sum(cached, axis=-1, keepdims=True) + (fresh0 + fresh1)
        mixture = lax.dot_general(
            (cached / totals).astype(BF16),
            s.vc[:, :, head],
            (((2,), (1,)), ((0,), (0,))),
            preferred_element_type=F32,
        ).reshape(shape)
        weight0 = (fresh0 / totals).astype(BF16).astype(F32).reshape(requests, 2, group, 1)
        weight1 = (fresh1 / totals).astype(BF16).astype(F32).reshape(requests, 2, group, 1)
        mixture = mixture + (weight0 * v[:, 0:1] + weight1 * v[:, 1:2])
        s.q3[...] = mixture.reshape(rows, group, HEAD_SIZE)
        for h in range(group):
            at = g * group_cols + h * HEAD_SIZE
            s.att[e, :, at : at + HEAD_SIZE] = s.q3[:, h, :].astype(BF16)
        if paired:
            g_copy(2, g).start()
            g_copy(1, g).start()
        else:
            each(n, lambda i: g_copy(i, g).start())

    piece = min(chunk, out_cols)
    pieces = out_cols // piece

    def place(block, index):
        return (
            pl.ds(pl.multiple_of(lax.div(index, 2) * half_rows, half_rows), half_rows),
            pl.ds(
                pl.multiple_of(block * out_cols + lax.rem(index, 2) * half_out, 128), half_out
            ),
        )

    def one_copy(i, j):
        p = tp_up(j)
        return remote(
            s.one_send.at[i, p], s.one_recv.at[i, j], s.o_s.at[i, j], s.o_r.at[i, j], tp=p
        )

    def three_copy(i):
        p = partner(i)
        return remote(
            s.three_send.at[i], s.out.at[place(e, t)], s.h_s.at[i], s.h_r.at[i], ep=p
        )

    def four_copy(i, j, index):
        ref = s.out.at[place(partner(i), index)]
        return remote(ref, ref, s.r_s.at[i, j], s.r_r.at[i, j], tp=tp_up(j))

    def project_head(i, g):
        values = s.att[partner(i), :, g * group_cols : (g + 1) * group_cols]
        for c in range(pieces):
            columns = slice(c * piece, (c + 1) * piece)
            value = dot(values, s.wo[g * group_cols : (g + 1) * group_cols, columns])
            if g > 0:
                value = s.acc[i, :, columns] + value
            s.acc[i, :, columns] = value

    def project_first(i):
        for g in range(kv_heads - 1):
            g_wait(i, g)
            project_head(i, g)

    def project(i, own=False):
        if not own:
            g_wait(i, kv_heads - 1)
        project_head(i, kv_heads - 1)
        for index in range(TP):
            k, side = index // 2, index % 2
            s.one_send[i, index] = s.acc[
                i,
                k * half_rows : (k + 1) * half_rows,
                side * half_out : (side + 1) * half_out,
            ].astype(BF16)
        for j in range(1, TP):
            one_copy(i, j).start()

    def add_up(i, own=False):
        value = s.acc[
            i,
            pl.ds(pl.multiple_of(b1 * half_rows, half_rows), half_rows),
            pl.ds(pl.multiple_of(b0 * half_out, 128), half_out),
        ]
        for j in range(1, TP):
            one_copy(i, j).wait_recv()
            value = value + s.one_recv[i, j].astype(F32)
        value = value.astype(BF16)
        if own:
            s.out[place(e, t)] = value
        else:
            s.three_send[i] = value
            three_copy(i).start()

    def pass_on(i, own=False):
        if not own:
            ref = s.out.at[place(partner(i), t)]
            remote(ref, ref, s.h_s.at[i], s.h_r.at[i], ep=partner(i)).wait_recv()
        for j in range(1, TP):
            four_copy(i, j, t).start()

    for g in range(kv_heads):
        attend(g)
        if g == 0:
            loads["wo"].wait()
        if g < kv_heads - 1:
            project_head(0, g)
    project(0, own=True)
    if paired:
        project_first(2)
        project_first(1)
        add_up(0, own=True)
        project_first(3)
        project(2)
        pass_on(0, own=True)
        project(1)
        add_up(2)
        project(3)
        add_up(1)
        pass_on(2)
        add_up(3)
        pass_on(1)
        pass_on(3)
    else:
        each(n, project_first)
        each(n, project)
        add_up(0, own=True)
        each(n, add_up)
        pass_on(0, own=True)
        each(n, pass_on)

    def last(i):
        for j in range(1, TP):
            four_copy(i, j, tp_down(j)).wait_recv()

    last(0)
    each(n, last)
    final = pltpu.make_async_copy(s.out, s.out_hbm, s.load_sem.at[0])
    final.start()

    def drain(i):
        a_copy(i).wait_send()
        m_copy(i).wait_send()
        b_copy(i).wait_send()
        for c in range(q_chunks + kv_chunks):
            p_copy(i, c).wait_send()
        for g in range(kv_heads):
            g_copy(i, g).wait_send()
        three_copy(i).wait_send()
        for k in range(3):
            f_copy(i, k, t).wait_send()

    each(n, drain)

    def drain_tp(i):
        for j in range(1, TP):
            one_copy(i, j).wait_send()
            four_copy(i, j, t).wait_send()

    drain_tp(0)
    each(n, drain_tp)
    for j in range(1, TP):
        s_copy(j).wait_send()
    final.wait()


def local(
    tokens,
    query_weight,
    key_weight,
    value_weight,
    output_weight,
    adapter_down_maps,
    adapter_up_maps,
    rotated_cache_keys,
    cached_value_rows,
    adapter_index,
    cached_lengths,
):
    n = lax.axis_size("ep")
    requests, steps, width = tokens.shape
    rows = requests * steps
    feat, q_cols = query_weight.shape
    kv_cols = key_weight.shape[1]
    all_cols = q_cols + 2 * kv_cols
    out_cols = output_weight.shape[1]
    half_out = out_cols // 2
    adapters, part, rank = adapter_down_maps.shape
    capacity = max(2, (2 * requests + n - 1) // n)
    slot_rows = max(16, -(-capacity * steps // 16) * 16)
    slots = n * slot_rows
    group = QUERY_HEADS // KEY_HEADS
    kv_heads = kv_cols // HEAD_SIZE
    chunks = all_cols // 512
    vmem = pltpu.VMEM
    dma = pltpu.SemaphoreType.DMA
    scratch = dict(
        tok=vmem((rows, width), BF16),
        nrm=vmem((rows, width), BF16),
        wq=vmem(query_weight.shape, BF16),
        wkv=vmem((feat, 2 * kv_cols), BF16),
        wo=vmem(output_weight.shape, BF16),
        dn=vmem((adapters, rank, part), BF16),
        up=vmem(adapter_up_maps.shape, BF16),
        kc=vmem(rotated_cache_keys.shape, BF16),
        vc=vmem(cached_value_rows.shape, BF16),
        x=vmem((n, rows, feat), BF16),
        b_send=vmem((n, slot_rows, part), BF16),
        b_recv=vmem((n, slot_rows, part), BF16),
        id_send=vmem((8, 128), jnp.int32),
        ids=vmem((n, 8, 128), jnp.int32),
        sh_send=vmem((slots, 128), F32),
        sh_recv=vmem((TP, slots, 128), F32),
        p_wide=vmem((n * rows, all_cols), F32),
        p_send=vmem((n, rows, all_cols), BF16),
        p_recv=vmem((n, rows, all_cols), BF16),
        tot=vmem((rows, all_cols), F32),
        cos=vmem((rows, HEAD_SIZE), F32),
        sin=vmem((rows, HEAD_SIZE), F32),
        lengths=vmem((requests, 2 * group, HEAD_SIZE), jnp.int32),
        q3=vmem((rows, group, HEAD_SIZE), F32),
        k3=vmem((rows, group, HEAD_SIZE), F32),
        v3=vmem((rows, group, HEAD_SIZE), F32),
        att=vmem((n, rows, q_cols), BF16),
        acc=vmem((n, rows, out_cols), F32),
        one_send=vmem((n, TP, rows // 2, half_out), BF16),
        one_recv=vmem((n, TP, rows // 2, half_out), BF16),
        three_send=vmem((n, rows // 2, half_out), BF16),
        out=vmem((rows, width), BF16),
        load_sem=dma((9,)),
        a_s=dma((n,)),
        a_r=dma((n,)),
        m_s=dma((n,)),
        m_r=dma((n,)),
        b_s=dma((n,)),
        b_r=dma((n,)),
        f_s=dma((n, 3)),
        f_r=dma((n, 3)),
        s_s=dma((TP,)),
        s_r=dma((TP,)),
        p_s=dma((n, chunks)),
        p_r=dma((n, chunks)),
        g_s=dma((n, kv_heads)),
        g_r=dma((n, kv_heads)),
        o_s=dma((n, TP)),
        o_r=dma((n, TP)),
        h_s=dma((n,)),
        h_r=dma((n,)),
        r_s=dma((n, TP)),
        r_r=dma((n, TP)),
    )
    operands = [
        "idx_ref",
        "len_ref",
        "tok_hbm",
        "wq_hbm",
        "wk_hbm",
        "wv_hbm",
        "wo_hbm",
        "dn_hbm",
        "up_hbm",
        "kc_hbm",
        "vc_hbm",
        "out_hbm",
    ]
    out = pl.pallas_call(
        functools.partial(body, n, operands + list(scratch)),
        out_shape=jax.ShapeDtypeStruct((rows, width), BF16),
        in_specs=[pl.BlockSpec(memory_space=pltpu.SMEM)] * 2
        + [pl.BlockSpec(memory_space=pl.ANY)] * 9,
        out_specs=pl.BlockSpec(memory_space=pl.ANY),
        scratch_shapes=list(scratch.values()),
        compiler_params=pltpu.CompilerParams(
            collective_id=0, has_side_effects=True, vmem_limit_bytes=60 * 2**20
        ),
        name="sublayer",
    )(
        adapter_index,
        cached_lengths,
        tokens.reshape(rows, width),
        query_weight,
        key_weight,
        value_weight,
        output_weight,
        jnp.swapaxes(adapter_down_maps, 1, 2),
        adapter_up_maps,
        rotated_cache_keys,
        cached_value_rows,
    )
    return out.reshape(tokens.shape)


def solution(mesh):
    return jax.shard_map(
        local,
        mesh=mesh,
        in_specs=(
            P(("groups", "ep"), None, None),
            P("ep", "tp"),
            P("ep", "tp"),
            P("ep", "tp"),
            P("tp", "ep"),
            P("ep", "tp", None),
            P("ep", None, "tp"),
            P(("groups", "ep"), None, "tp"),
            P(("groups", "ep"), None, "tp"),
            P(("groups", "ep")),
            P(("groups", "ep")),
        ),
        out_specs=P(("groups", "ep"), None, None),
        check_vma=False,
    )
```

```python
import functools
import math
import types

import jax
import jax.numpy as jnp
from jax import lax
from jax.experimental import pallas as pl
from jax.experimental.pallas import tpu as pltpu
from jax.sharding import PartitionSpec as P

QUERY_HEADS = 64
KEY_HEADS = 8
HEAD_SIZE = 128
EPSILON = 1e-05
THETA = 500000.0
MASKED = -1e30
MESH = pl.DeviceIdType.MESH
F32 = jnp.float32
BF16 = jnp.bfloat16
TP = 4
UNROLL_PEERS = 8


def each(count, body):
    if count <= UNROLL_PEERS:
        for i in range(1, count):
            body(i)
    else:

        @pl.loop(1, count)
        def _(i):
            body(i)


def dot(a, b):
    return jnp.dot(a, b, preferred_element_type=F32)


def body(n, names, *refs):
    s = types.SimpleNamespace(**dict(zip(names, refs)))
    e = lax.axis_index("ep")
    t = lax.axis_index("tp")
    rows, width = s.tok.shape
    requests = rows // 2
    half_rows = rows // 2
    feat = width // n
    half_feat = feat // 2
    slot_rows = s.b_recv.shape[1]
    part = s.b_recv.shape[2]
    q_cols = s.wq.shape[1]
    kv_cols = s.wkv.shape[1] // 2
    out_cols = s.wo.shape[1]
    half_out = out_cols // 2
    adapters = s.dn.shape[0]
    rank = s.dn.shape[1]
    kv_heads = kv_cols // HEAD_SIZE
    group = QUERY_HEADS // KEY_HEADS
    chunk = 512
    group_cols = group * HEAD_SIZE

    def partner(i):
        both = 0
        bit = 1
        while bit < n:
            both = both + bit * (lax.rem(lax.div(e, bit), 2) * ((i // bit) % 2))
            bit *= 2
        return e + i - 2 * both

    def tp_up(j):
        return lax.rem(t + j, TP)

    def tp_down(j):
        return lax.rem(t + TP - j, TP)

    def remote(src, dst, send, recv, ep=None, tp=None):
        return pltpu.make_async_remote_copy(
            src_ref=src,
            dst_ref=dst,
            send_sem=send,
            recv_sem=recv,
            device_id={"ep": e if ep is None else ep, "tp": t if tp is None else tp},
            device_id_type=MESH,
        )

    loads = {}
    for k, (name, src, dst) in enumerate(
        [
            ("tok", s.tok_hbm, s.tok),
            ("dn", s.dn_hbm, s.dn),
            ("wk", s.wk_hbm, s.wkv.at[:, :kv_cols]),
            ("wv", s.wv_hbm, s.wkv.at[:, kv_cols:]),
            ("wq", s.wq_hbm, s.wq),
            ("up", s.up_hbm, s.up),
            ("kc", s.kc_hbm, s.kc),
            ("vc", s.vc_hbm, s.vc),
            ("wo", s.wo_hbm, s.wo),
        ]
    ):
        loads[name] = pltpu.make_async_copy(src, dst, s.load_sem.at[k])
        loads[name].start()

    barrier = pltpu.get_barrier_semaphore()

    def greet(i):
        pl.semaphore_signal(
            barrier, inc=1, device_id={"ep": partner(i), "tp": t}, device_id_type=MESH
        )

    each(n, greet)
    for j in range(1, TP):
        pl.semaphore_signal(
            barrier, inc=1, device_id={"ep": e, "tp": tp_up(j)}, device_id_type=MESH
        )

    square = (1, rows, rows)
    sub = lax.broadcasted_iota(jnp.int32, square, 1)
    lane = lax.broadcasted_iota(jnp.int32, square, 2)
    sub_req = jnp.right_shift(sub, 1)
    lane_req = jnp.right_shift(lane, 1)
    slots = n * slot_rows

    def slots_of(flags):
        flags_sub = jnp.sum(jnp.where(sub == lane, flags, 0), axis=2, keepdims=True)
        before_lane = jnp.sum(jnp.where(sub_req < lane_req, flags_sub, 0), axis=1, keepdims=True)
        before_sub = jnp.sum(jnp.where(lane_req < sub_req, flags, 0), axis=2, keepdims=True)
        return (
            flags_sub,
            before_lane + (lane - 2 * lane_req)[:, :1],
            before_sub + (sub - 2 * sub_req)[:, :, :1],
        )

    tile_req = jnp.right_shift(lax.broadcasted_iota(jnp.int32, (8, 128), 1), 1)
    lane3 = lax.broadcasted_iota(jnp.int32, (rows, HEAD_SIZE), 0)
    position = jnp.zeros((rows, HEAD_SIZE), F32)
    own_ids = jnp.zeros((8, 128), jnp.int32)
    for r in range(requests):
        own_ids = jnp.where(tile_req == r, s.idx_ref[r], own_ids)
        length = s.len_ref[r]
        s.lengths[r] = jnp.full((2 * group, HEAD_SIZE), length, jnp.int32)
        position = jnp.where(jnp.right_shift(lane3, 1) == r, length.astype(F32), position)
    position = position + (lane3 - 2 * jnp.right_shift(lane3, 1)).astype(F32)
    s.id_send[...] = own_ids
    s.ids[e] = own_ids
    owners = lax.broadcasted_iota(jnp.int32, (n, 1, rows), 0)
    own_row = own_ids[:1, :rows].reshape(1, 1, rows) - owners * adapters
    flags = jnp.where((own_row >= 0) & (own_row < adapters), 1, 0)
    _, slot_lane, _ = slots_of(flags)
    placing = (lax.broadcasted_iota(jnp.int32, (n, slot_rows, rows), 1) == slot_lane) & (flags > 0)
    placing = jnp.where(placing, 1.0, 0.0).reshape(slots, rows)

    loads["tok"].wait()
    for r in range(0, rows, 16):
        wide = s.tok[r : r + 16, :].astype(F32)
        factor = lax.rsqrt(jnp.mean(wide * wide, axis=-1, keepdims=True) + EPSILON)
        s.nrm[r : r + 16, :] = (wide * factor).astype(BF16)

    pl.semaphore_wait(barrier, n - 1 + TP - 1)

    def quarter(block, index):
        return (
            block,
            pl.ds(pl.multiple_of(lax.rem(index, 2) * half_rows, half_rows), half_rows),
            pl.ds(pl.multiple_of(lax.div(index, 2) * half_feat, 128), half_feat),
        )

    def a_copy(i):
        p = partner(i)
        src = s.nrm.at[
            pl.ds(pl.multiple_of(lax.rem(t, 2) * half_rows, half_rows), half_rows),
            pl.ds(pl.multiple_of(p * feat + lax.div(t, 2) * half_feat, 128), half_feat),
        ]
        return remote(src, s.x.at[quarter(e, t)], s.a_s.at[i], s.a_r.at[i], ep=p)

    each(n, lambda i: a_copy(i).start())

    def m_copy(i):
        p = partner(i)
        return remote(s.id_send, s.ids.at[e], s.m_s.at[i], s.m_r.at[i], ep=p)

    each(n, lambda i: m_copy(i).start())

    own_part = s.nrm[:, pl.ds(pl.multiple_of(t * part, 128), part)]
    placed = dot(placing.astype(BF16), own_part).astype(BF16)
    s.b_send[...] = placed.reshape(n, slot_rows, part)

    def b_copy(i):
        p = partner(i)
        return remote(s.b_send.at[p], s.b_recv.at[e], s.b_s.at[i], s.b_r.at[i], ep=p)

    each(n, lambda i: b_copy(i).start())
    s.b_recv[e] = s.b_send[e]
    s.x[e] = s.nrm[:, pl.ds(pl.multiple_of(e * feat, 128), feat)]

    pair = lax.broadcasted_iota(jnp.int32, (rows, HEAD_SIZE), 1)
    upper = pair >= HEAD_SIZE // 2
    pair = jnp.where(upper, pair - HEAD_SIZE // 2, pair).astype(F32)
    angles = position * jnp.exp(pair * (-2.0 / HEAD_SIZE) * math.log(THETA))
    s.cos[...] = jnp.cos(angles)
    sine = jnp.sin(angles)
    s.sin[...] = jnp.where(upper, sine, -sine)

    b0 = lax.rem(t, 2)
    b1 = lax.div(t, 2)
    near = t + 1 - 2 * b0
    far = t + 2 - 4 * b1
    across = near + 2 - 4 * b1

    def f_copy(i, k, index):
        ref = s.x.at[quarter(partner(i), index)]
        return remote(ref, ref, s.f_s.at[i, k], s.f_r.at[i, k], tp=far if k == 1 else near)

    def forward(i):
        ref = s.x.at[quarter(partner(i), t)]
        remote(ref, ref, s.a_s.at[i], s.a_r.at[i], ep=partner(i)).wait_recv()
        f_copy(i, 1, t).start()
        f_copy(i, 0, t).start()

    def forward_far(i):
        f_copy(i, 1, far).wait_recv()
        f_copy(i, 2, far).start()

    each(n, forward)
    each(n, forward_far)

    def f_in(i):
        f_copy(i, 0, near).wait_recv()
        f_copy(i, 2, across).wait_recv()

    each(n, f_in)
    loads["wk"].wait()
    loads["wv"].wait()
    row_block = s.x[...].reshape(n * rows, feat)

    paired = n == 4

    def p_copy(i, c):
        p = partner(i)
        columns = pl.ds(c * chunk, chunk)
        return remote(
            s.p_send.at[p, :, columns],
            s.p_recv.at[i, :, columns],
            s.p_s.at[i, c],
            s.p_r.at[i, c],
            ep=partner(1) if paired and i == 3 else p,
        )

    def ship(c, value):
        columns = slice(c * chunk, (c + 1) * chunk)
        s.p_wide[:, columns] = value
        s.p_send[:, :, columns] = value.astype(BF16).reshape(n, rows, chunk)
        if paired:
            p_copy(1, c).start()
            p_copy(3, c).start()
        else:
            each(n, lambda i: p_copy(i, c).start())

    def ship_far(c):
        columns = slice(c * chunk, (c + 1) * chunk)
        p_copy(3, c).wait_recv()
        p = partner(2)
        value = s.p_wide[pl.ds(pl.multiple_of(p * rows, rows), rows), columns]
        value = value + s.p_recv[3, :, columns].astype(F32)
        s.p_send[p, :, columns] = value.astype(BF16)
        p_copy(2, c).start()

    q_chunks = q_cols // chunk
    kv_chunks = 2 * kv_cols // chunk
    for c in range(kv_chunks):
        ship(q_chunks + c, dot(row_block, s.wkv[:, c * chunk : (c + 1) * chunk]))

    loads["wq"].wait()
    for c in range(q_chunks):
        columns = slice(c * chunk, (c + 1) * chunk)
        s.p_wide[:, columns] = dot(row_block, s.wq[:, columns])

    def b_in(i):
        m_copy(i).wait_recv()
        remote(
            s.b_send.at[partner(i)],
            s.b_recv.at[partner(i)],
            s.b_s.at[i],
            s.b_r.at[i],
            ep=partner(i),
        ).wait_recv()

    each(n, b_in)
    loads["dn"].wait()
    arrived = s.b_recv[...].reshape(slots, part)
    ids = s.ids[:, :1, :rows] - e * adapters
    flags = jnp.where((ids >= 0) & (ids < adapters), 1, 0)
    flags_sub, slot_lane, slot_sub = slots_of(flags)
    taken = (lax.broadcasted_iota(jnp.int32, (n, slot_rows, rows), 1) == slot_lane) & (flags > 0)
    labels = jnp.sum(jnp.where(taken, ids, 0), axis=2, keepdims=True)
    labels = jnp.broadcast_to(labels, (n, slot_rows, 128)).reshape(slots, 128)
    lane_slot = lax.broadcasted_iota(jnp.int32, (slots, 128), 1)
    offset = jnp.where(lane_slot >= rank, 1, 0)
    down = lax.dot_general(
        arrived,
        s.dn[...].reshape(adapters * rank, part),
        (((1,), (1,)), ((), ())),
        preferred_element_type=F32,
    )
    total = jnp.zeros((slots, 128), F32)
    for a in range(adapters // 2):
        block = down[:, 128 * a : 128 * (a + 1)]
        total = total + jnp.where(labels == 2 * a + offset, block, 0.0)
    s.sh_send[...] = total + pltpu.roll(total, rank, 1)

    def s_copy(j):
        return remote(s.sh_send, s.sh_recv.at[j], s.s_s.at[j], s.s_r.at[j], tp=tp_up(j))

    for j in range(1, TP):
        s_copy(j).start()

    if paired:
        for c in range(kv_chunks):
            ship_far(q_chunks + c)

    for j in range(1, TP):
        s_copy(j).wait_recv()
        total_j = s.sh_recv[j]
        sh = s.sh_send[...] + total_j if j == 1 else sh + total_j
    sh = sh.astype(BF16)
    spread = jnp.concatenate(
        [
            jnp.where(labels == 2 * a + offset, sh, jnp.zeros_like(sh))
            for a in range(adapters // 2)
        ],
        axis=1,
    )
    loads["up"].wait()
    block = lax.broadcasted_iota(jnp.int32, (n, rows, 1), 0) * slot_rows
    codes = jnp.where(flags_sub > 0, slot_sub + block, -1)
    returning = lax.broadcasted_iota(jnp.int32, (n, rows, slots), 2) == codes
    returning = jnp.where(returning, 1.0, 0.0).reshape(n * rows, slots).astype(BF16)
    up = s.up[...].reshape(adapters * rank, q_cols)
    for c in range(q_chunks):
        columns = slice(c * chunk, (c + 1) * chunk)
        delta = dot(spread, up[:, columns]).astype(BF16)
        ship(c, s.p_wide[:, columns] + dot(returning, delta))
    if paired:
        for c in range(q_chunks):
            ship_far(c)

    def p_sum(c):
        columns = slice(c * chunk, (c + 1) * chunk)
        sources = range(1, 3 if paired else n)
        if paired:
            for i in sources:
                p_copy(i, c).wait_recv()
        else:
            each(n, lambda i: p_copy(i, c).wait_recv())
        value = s.p_wide[pl.ds(pl.multiple_of(e * rows, rows), rows), columns]
        for i in sources:
            value = value + s.p_recv[i, :, columns].astype(F32)
        s.tot[:, columns] = value

    def rotate(value):
        return (value * s.cos[...] + pltpu.roll(value, HEAD_SIZE // 2, 1) * s.sin[...]).astype(BF16)

    for c in range(kv_chunks):
        p_sum(q_chunks + c)
    loads["kc"].wait()
    loads["vc"].wait()
    scale = 1.0 / math.sqrt(HEAD_SIZE)
    shape = (requests, 2, group, HEAD_SIZE)
    flat = (requests, 2 * group, HEAD_SIZE)
    slots_lane = lax.broadcasted_iota(jnp.int32, flat, 2)
    second = lax.broadcasted_iota(jnp.int32, (requests, 2, group, 1), 1) == 1

    def g_copy(i, g):
        columns = pl.ds(g * group_cols, group_cols)
        if paired and i == 3:
            ref = s.att.at[partner(2), :, columns]
            return remote(ref, ref, s.g_s.at[i, g], s.g_r.at[i, g], ep=partner(1))
        ref = s.att.at[e, :, columns]
        return remote(ref, ref, s.g_s.at[i, g], s.g_r.at[i, g], ep=partner(i))

    def g_wait(i, g):
        g_copy(i, g).wait_recv()
        if paired and i == 2:
            g_copy(3, g).start()

    def attend(g):
        for c in range(g * group_cols // chunk, (g + 1) * group_cols // chunk):
            p_sum(c)
        base = q_cols + g * HEAD_SIZE
        key = rotate(s.tot[:, base : base + HEAD_SIZE]).astype(F32)
        value = s.tot[:, base + kv_cols : base + kv_cols + HEAD_SIZE].astype(BF16).astype(F32)
        for h in range(group):
            at = g * group_cols + h * HEAD_SIZE
            s.q3[:, h, :] = rotate(s.tot[:, at : at + HEAD_SIZE]).astype(F32)
            s.k3[:, h, :] = key
            s.v3[:, h, :] = value
        q = s.q3[...].reshape(shape)
        k = s.k3[...].reshape(shape)
        v = s.v3[...].reshape(shape)
        head = slice(g * HEAD_SIZE, (g + 1) * HEAD_SIZE)
        cached = lax.dot_general(
            q.reshape(flat).astype(BF16),
            s.kc[:, :, head],
            (((2,), (2,)), ((0,), (0,))),
            preferred_element_type=F32,
        )
        live = slots_lane < s.lengths[...]
        cached = jnp.where(live, cached * scale, MASKED)
        fresh0 = jnp.sum(q * k[:, 0:1], axis=-1, keepdims=True) * scale
        fresh1 = jnp.sum(q * k[:, 1:2], axis=-1, keepdims=True) * scale
        fresh1 = jnp.where(second, fresh1, MASKED)
        fresh0 = fresh0.reshape(requests, 2 * group, 1)
        fresh1 = fresh1.reshape(requests, 2 * group, 1)
        top = jnp.maximum(
            jnp.max(cached, axis=-1, keepdims=True), jnp.maximum(fresh0, fresh1)
        )
        cached = jnp.where(live, jnp.exp(cached - top), 0.0)
        fresh0 = jnp.exp(fresh0 - top)
        fresh1 = jnp.where(second.reshape(requests, 2 * group, 1), jnp.exp(fresh1 - top), 0.0)
        totals = jnp.sum(cached, axis=-1, keepdims=True) + (fresh0 + fresh1)
        mixture = lax.dot_general(
            (cached / totals).astype(BF16),
            s.vc[:, :, head],
            (((2,), (1,)), ((0,), (0,))),
            preferred_element_type=F32,
        ).reshape(shape)
        weight0 = (fresh0 / totals).astype(BF16).astype(F32).reshape(requests, 2, group, 1)
        weight1 = (fresh1 / totals).astype(BF16).astype(F32).reshape(requests, 2, group, 1)
        mixture = mixture + (weight0 * v[:, 0:1] + weight1 * v[:, 1:2])
        s.q3[...] = mixture.reshape(rows, group, HEAD_SIZE)
        for h in range(group):
            at = g * group_cols + h * HEAD_SIZE
            s.att[e, :, at : at + HEAD_SIZE] = s.q3[:, h, :].astype(BF16)
        if paired:
            g_copy(2, g).start()
            g_copy(1, g).start()
        else:
            each(n, lambda i: g_copy(i, g).start())

    piece = min(chunk, out_cols)
    pieces = out_cols // piece

    def place(block, index):
        return (
            pl.ds(pl.multiple_of(lax.div(index, 2) * half_rows, half_rows), half_rows),
            pl.ds(
                pl.multiple_of(block * out_cols + lax.rem(index, 2) * half_out, 128), half_out
            ),
        )

    def one_copy(i, j):
        p = tp_up(j)
        return remote(
            s.one_send.at[i, p], s.one_recv.at[i, j], s.o_s.at[i, j], s.o_r.at[i, j], tp=p
        )

    def three_copy(i):
        p = partner(i)
        return remote(
            s.three_send.at[i], s.out.at[place(e, t)], s.h_s.at[i], s.h_r.at[i], ep=p
        )

    def four_copy(i, j, index):
        ref = s.out.at[place(partner(i), index)]
        return remote(ref, ref, s.r_s.at[i, j], s.r_r.at[i, j], tp=tp_up(j))

    def project_head(i, g):
        values = s.att[partner(i), :, g * group_cols : (g + 1) * group_cols]
        for c in range(pieces):
            columns = slice(c * piece, (c + 1) * piece)
            value = dot(values, s.wo[g * group_cols : (g + 1) * group_cols, columns])
            if g > 0:
                value = s.acc[i, :, columns] + value
            s.acc[i, :, columns] = value

    def project_first(i):
        for g in range(kv_heads - 1):
            g_wait(i, g)
            project_head(i, g)

    def project(i, own=False):
        if not own:
            g_wait(i, kv_heads - 1)
        project_head(i, kv_heads - 1)
        for index in range(TP):
            k, side = index // 2, index % 2
            s.one_send[i, index] = s.acc[
                i,
                k * half_rows : (k + 1) * half_rows,
                side * half_out : (side + 1) * half_out,
            ].astype(BF16)
        for j in range(1, TP):
            one_copy(i, j).start()

    def add_up(i, own=False):
        value = s.acc[
            i,
            pl.ds(pl.multiple_of(b1 * half_rows, half_rows), half_rows),
            pl.ds(pl.multiple_of(b0 * half_out, 128), half_out),
        ]
        for j in range(1, TP):
            one_copy(i, j).wait_recv()
            value = value + s.one_recv[i, j].astype(F32)
        value = value.astype(BF16)
        if own:
            s.out[place(e, t)] = value
        else:
            s.three_send[i] = value
            three_copy(i).start()

    def pass_on(i, own=False):
        if not own:
            ref = s.out.at[place(partner(i), t)]
            remote(ref, ref, s.h_s.at[i], s.h_r.at[i], ep=partner(i)).wait_recv()
        for j in range(1, TP):
            four_copy(i, j, t).start()

    for g in range(kv_heads):
        attend(g)
        if g == 0:
            loads["wo"].wait()
        if g < kv_heads - 1:
            project_head(0, g)
    project(0, own=True)
    if paired:
        project_first(2)
        project_first(1)
        add_up(0, own=True)
        project_first(3)
        project(2)
        pass_on(0, own=True)
        project(1)
        project(3)
        add_up(2)
        add_up(1)
        pass_on(2)
        add_up(3)
        pass_on(1)
        pass_on(3)
    else:
        each(n, project_first)
        each(n, project)
        add_up(0, own=True)
        each(n, add_up)
        pass_on(0, own=True)
        each(n, pass_on)

    def last(i):
        for j in range(1, TP):
            four_copy(i, j, tp_down(j)).wait_recv()

    last(0)
    each(n, last)
    final = pltpu.make_async_copy(s.out, s.out_hbm, s.load_sem.at[0])
    final.start()

    def drain(i):
        a_copy(i).wait_send()
        m_copy(i).wait_send()
        b_copy(i).wait_send()
        for c in range(q_chunks + kv_chunks):
            p_copy(i, c).wait_send()
        for g in range(kv_heads):
            g_copy(i, g).wait_send()
        three_copy(i).wait_send()
        for k in range(3):
            f_copy(i, k, t).wait_send()

    each(n, drain)

    def drain_tp(i):
        for j in range(1, TP):
            one_copy(i, j).wait_send()
            four_copy(i, j, t).wait_send()

    drain_tp(0)
    each(n, drain_tp)
    for j in range(1, TP):
        s_copy(j).wait_send()
    final.wait()


def local(
    tokens,
    query_weight,
    key_weight,
    value_weight,
    output_weight,
    adapter_down_maps,
    adapter_up_maps,
    rotated_cache_keys,
    cached_value_rows,
    adapter_index,
    cached_lengths,
):
    n = lax.axis_size("ep")
    requests, steps, width = tokens.shape
    rows = requests * steps
    feat, q_cols = query_weight.shape
    kv_cols = key_weight.shape[1]
    all_cols = q_cols + 2 * kv_cols
    out_cols = output_weight.shape[1]
    half_out = out_cols // 2
    adapters, part, rank = adapter_down_maps.shape
    capacity = max(2, (2 * requests + n - 1) // n)
    slot_rows = max(16, -(-capacity * steps // 16) * 16)
    slots = n * slot_rows
    group = QUERY_HEADS // KEY_HEADS
    kv_heads = kv_cols // HEAD_SIZE
    chunks = all_cols // 512
    vmem = pltpu.VMEM
    dma = pltpu.SemaphoreType.DMA
    scratch = dict(
        tok=vmem((rows, width), BF16),
        nrm=vmem((rows, width), BF16),
        wq=vmem(query_weight.shape, BF16),
        wkv=vmem((feat, 2 * kv_cols), BF16),
        wo=vmem(output_weight.shape, BF16),
        dn=vmem((adapters, rank, part), BF16),
        up=vmem(adapter_up_maps.shape, BF16),
        kc=vmem(rotated_cache_keys.shape, BF16),
        vc=vmem(cached_value_rows.shape, BF16),
        x=vmem((n, rows, feat), BF16),
        b_send=vmem((n, slot_rows, part), BF16),
        b_recv=vmem((n, slot_rows, part), BF16),
        id_send=vmem((8, 128), jnp.int32),
        ids=vmem((n, 8, 128), jnp.int32),
        sh_send=vmem((slots, 128), F32),
        sh_recv=vmem((TP, slots, 128), F32),
        p_wide=vmem((n * rows, all_cols), F32),
        p_send=vmem((n, rows, all_cols), BF16),
        p_recv=vmem((n, rows, all_cols), BF16),
        tot=vmem((rows, all_cols), F32),
        cos=vmem((rows, HEAD_SIZE), F32),
        sin=vmem((rows, HEAD_SIZE), F32),
        lengths=vmem((requests, 2 * group, HEAD_SIZE), jnp.int32),
        q3=vmem((rows, group, HEAD_SIZE), F32),
        k3=vmem((rows, group, HEAD_SIZE), F32),
        v3=vmem((rows, group, HEAD_SIZE), F32),
        att=vmem((n, rows, q_cols), BF16),
        acc=vmem((n, rows, out_cols), F32),
        one_send=vmem((n, TP, rows // 2, half_out), BF16),
        one_recv=vmem((n, TP, rows // 2, half_out), BF16),
        three_send=vmem((n, rows // 2, half_out), BF16),
        out=vmem((rows, width), BF16),
        load_sem=dma((9,)),
        a_s=dma((n,)),
        a_r=dma((n,)),
        m_s=dma((n,)),
        m_r=dma((n,)),
        b_s=dma((n,)),
        b_r=dma((n,)),
        f_s=dma((n, 3)),
        f_r=dma((n, 3)),
        s_s=dma((TP,)),
        s_r=dma((TP,)),
        p_s=dma((n, chunks)),
        p_r=dma((n, chunks)),
        g_s=dma((n, kv_heads)),
        g_r=dma((n, kv_heads)),
        o_s=dma((n, TP)),
        o_r=dma((n, TP)),
        h_s=dma((n,)),
        h_r=dma((n,)),
        r_s=dma((n, TP)),
        r_r=dma((n, TP)),
    )
    operands = [
        "idx_ref",
        "len_ref",
        "tok_hbm",
        "wq_hbm",
        "wk_hbm",
        "wv_hbm",
        "wo_hbm",
        "dn_hbm",
        "up_hbm",
        "kc_hbm",
        "vc_hbm",
        "out_hbm",
    ]
    out = pl.pallas_call(
        functools.partial(body, n, operands + list(scratch)),
        out_shape=jax.ShapeDtypeStruct((rows, width), BF16),
        in_specs=[pl.BlockSpec(memory_space=pltpu.SMEM)] * 2
        + [pl.BlockSpec(memory_space=pl.ANY)] * 9,
        out_specs=pl.BlockSpec(memory_space=pl.ANY),
        scratch_shapes=list(scratch.values()),
        compiler_params=pltpu.CompilerParams(
            collective_id=0, has_side_effects=True, vmem_limit_bytes=60 * 2**20
        ),
        name="sublayer",
    )(
        adapter_index,
        cached_lengths,
        tokens.reshape(rows, width),
        query_weight,
        key_weight,
        value_weight,
        output_weight,
        jnp.swapaxes(adapter_down_maps, 1, 2),
        adapter_up_maps,
        rotated_cache_keys,
        cached_value_rows,
    )
    return out.reshape(tokens.shape)


def solution(mesh):
    return jax.shard_map(
        local,
        mesh=mesh,
        in_specs=(
            P(("groups", "ep"), None, None),
            P("ep", "tp"),
            P("ep", "tp"),
            P("ep", "tp"),
            P("tp", "ep"),
            P("ep", "tp", None),
            P("ep", None, "tp"),
            P(("groups", "ep"), None, "tp"),
            P(("groups", "ep"), None, "tp"),
            P(("groups", "ep")),
            P(("groups", "ep")),
        ),
        out_specs=P(("groups", "ep"), None, None),
        check_vma=False,
    )
```
